32 devices in a mesh: seq: 8 (over y, x, core), kv: 4 (over z).
Axes of the slice: x: 2, y: 2, z: 4, core: 2. Of those that a mesh axis runs over, the one named last changes fastest.
Arguments:
- src_embed: bfloat16 [2, 8, 256, 1024], P(None, 'seq', 'kv'), may hold values from -6 to 6
- tgt_embed: bfloat16 [2, 8, 512, 1024], P(None, 'seq', 'kv'), may hold values from -6 to 6
- targets: int32 [2, 8, 512], P(None, None, 'kv'), may hold values from 0 to 50271
- src_len: int32 [2, 8], replicated, may hold values from 64 to 256, as said below
- tgt_len: int32 [2, 8], replicated, may hold values from 64 to 512, as said below
- task: int32 [2, 8], replicated, may hold values from 0 to 1
- step: int32 [1], replicated, may hold values from 2 to 20
- attn_in: bfloat16 [3, 1024, 3072], P(None, ('seq', 'kv')), may hold values from -0.1875 to 0.1875
- attn_out: bfloat16 [3, 1024, 1024], P(None, ('seq', 'kv')), may hold values from -0.75 to 0.75
- ffn_in: bfloat16 [2, 1024, 4096], P(None, ('seq', 'kv')), may hold values from -0.1875 to 0.1875
- ffn_out: bfloat16 [2, 4096, 1024], P(None, ('seq', 'kv')), may hold values from -0.09375 to 0.09375
- embed: bfloat16 [50272, 1024], P('seq'), may hold values from -0.375 to 0.375
- down_w: float32 [2, 2, 1024, 512], P(None, None, ('seq', 'kv')), may hold values from -0.1875 to 0.1875
- down_m: float32 [2, 2, 1024, 512], P(None, None, ('seq', 'kv')), may hold values from -1.5258789e-05 to 1.5258789e-05
- down_v: float32 [2, 2, 1024, 512], P(None, None, ('seq', 'kv')), may hold values from 9.536743e-14 to 3.8146973e-13
- up_w: float32 [2, 2, 512, 1024], P(None, None, ('seq', 'kv')), may hold values from -0.0625 to 0.0625
- up_m: float32 [2, 2, 512, 1024], P(None, None, ('seq', 'kv')), may hold values from -1.5258789e-05 to 1.5258789e-05
- up_v: float32 [2, 2, 512, 1024], P(None, None, ('seq', 'kv')), may hold values from 9.536743e-14 to 3.8146973e-13
- norm_params: float32 [2, 7, 1024], replicated
- norm_m: float32 [2, 7, 1024], replicated, may hold values from -0.00012207031 to 0.00012207031
- norm_v: float32 [2, 7, 1024], replicated, may hold values from 6.9754463e-12 to 2.7901785e-11
Outputs:
- loss_sum: float32 [], replicated
- token_count: float32 [], replicated
- grad_norm: float32 [], replicated
- down_new: float32 [2, 2, 1024, 512], P(None, None, ('seq', 'kv'))
- down_m_new: float32 [2, 2, 1024, 512], P(None, None, ('seq', 'kv'))
- down_v_new: float32 [2, 2, 1024, 512], P(None, None, ('seq', 'kv'))
- up_new: float32 [2, 2, 512, 1024], P(None, None, ('seq', 'kv'))
- up_m_new: float32 [2, 2, 512, 1024], P(None, None, ('seq', 'kv'))
- up_v_new: float32 [2, 2, 512, 1024], P(None, None, ('seq', 'kv'))
- norm_new: float32 [2, 7, 1024], replicated
- norm_m_new: float32 [2, 7, 1024], replicated
- norm_v_new: float32 [2, 7, 1024], replicated
- norm_grad: float32 [2, 7, 1024], replicated
The draws below stay inside these ranges and needn't reach their ends.
Inputs may be any that keep to these rules, and one draw needn't show every extreme that they name: `src_len`: every micro-batch has an item of the full source length 256. `tgt_len`: every micro-batch has an item of the full target length 512.
All inputs are finite; a program needn't handle non-finite values.
Results may differ from the reference program's by a relative error of at most 0.005.
Values may be sent and summed in bfloat16 or wider, within the bound.
No kernel may reach another device: no remote copies, remote signals or barrier semaphores. Data moves between devices by JAX's collectives and lax.ppermute only.
A program may use at most 320 MiB of HBM per device.

```python
import math
import jax
import jax.numpy as jnp
import numpy as np
from jax import lax

D = 1024
FF = 4096
HDIM = 64
A = 512
VOCAB = 50272
TASKS = 2
MICRO = 2
GROUPS = 8
SRC = 256
TGT = 512


def ragged_lengths(key, salt, shortest, longest):
    first, second = jax.random.split(jax.random.fold_in(key, salt))
    lengths = jax.random.randint(first, (MICRO, GROUPS), shortest, longest + 1)
    chosen = jax.random.randint(second, (MICRO,), 0, GROUPS)
    marked = jnp.arange(GROUPS)[None, :] == chosen[:, None]
    return jnp.where(marked, longest, lengths).astype(jnp.int32)


def draw_src_len(key, part):
    return ragged_lengths(key, 11, SRC // 4, SRC)


def draw_tgt_len(key, part):
    return ragged_lengths(key, 23, TGT // 8, TGT)


def draw_embed(key, part):
    key = jax.random.fold_in(key, 41)
    ramp = jnp.arange(VOCAB, dtype=jnp.float32)[:, None] / (VOCAB - 1)
    base = jnp.clip(jax.random.normal(key, (VOCAB, D), jnp.float32), -4.0, 4.0)
    scale = 1.0 + 2.0 * ramp
    return (base * scale * D ** (-0.5)).astype(jnp.bfloat16)


def draw_norm_params(key, part):
    first, second = jax.random.split(jax.random.fold_in(key, 37))
    gains = 1.0 + 0.1 * jax.random.normal(first, (7, D), jnp.float32)
    biases = 0.1 * jax.random.normal(second, (7, D), jnp.float32)
    return jnp.stack([gains, biases]).astype(jnp.float32)


def plant(entries, stream_key, low, high):
    shape = entries.shape
    index_at = [jax.random.randint(jax.random.fold_in(stream_key, axis), (), 0, shape[axis]) for axis in range(len(shape))]
    entries = entries.at[tuple(index_at)].set(low)
    longest = shape.index(max(shape))
    index_at[longest] = (index_at[longest] + 1) % shape[longest]
    return entries.at[tuple(index_at)].set(high)


def levels(rng, extent, shards, low, largest):
    loudness = 1.0
    for position, parts in shards:
        heights = jax.random.uniform(jax.random.fold_in(jax.random.fold_in(rng, 6), position), (parts,), jnp.float32, low / len(shards), largest / len(shards))
        loudness = loudness * jnp.repeat(jnp.exp(heights), extent[position] // parts).reshape((-1,) + (1,) * (len(extent) - 1 - position))
    return loudness


def cumulative_ranks(count, lean):
    weights = [(1 << 20) // math.isqrt(standing ** lean) + 1 for standing in range(1, count + 1)]
    deviation = 1 + sum(weights) // (1 << 30)
    return np.cumsum(np.array([max(1, weight // deviation) for weight in weights]))


def ranked(rng, extent, number_of, slope):
    listing = cumulative_ranks(number_of, slope)
    pick = jax.random.randint(jax.random.fold_in(rng, 1), extent, 0, int(listing[number_of - 1]))
    rank = jnp.searchsorted(jnp.asarray(listing, jnp.int32), pick, side="right")
    return jax.random.permutation(jax.random.fold_in(rng, 2), number_of)[rank].astype(jnp.int32)


def normal_values(stream_key, extent, deviation, most, pieces=(), kind=jnp.bfloat16):
    array = deviation * jax.random.normal(stream_key, extent, jnp.float32)
    if pieces:
        array = array * levels(stream_key, extent, pieces, -0.22, 0.18)
    return jnp.clip(array, -most, most).astype(kind)


def setup_inputs(seed: int = 0) -> dict:
    splits = jax.random.split(jax.random.key(seed), 22)
    return {
        "src_embed": normal_values(splits[0], (MICRO, GROUPS, SRC, D), 1.0, 6.0, ((1, 8), (2, 4))),
        "tgt_embed": normal_values(splits[1], (MICRO, GROUPS, TGT, D), 1.0, 6.0, ((1, 8), (2, 4))),
        "targets": plant(ranked(splits[2], (MICRO, GROUPS, TGT), VOCAB, 2), jax.random.fold_in(splits[2], 3), 0, VOCAB - 1).astype(jnp.int32),
        "src_len": draw_src_len(jax.random.fold_in(splits[21], 71), 0),
        "tgt_len": draw_tgt_len(jax.random.fold_in(splits[21], 71), 0),
        "task": plant(jax.random.randint(splits[5], (MICRO, GROUPS), 0, TASKS), jax.random.fold_in(splits[5], 1), 0, TASKS - 1).astype(jnp.int32),
        "step": jax.random.randint(splits[6], (1,), 2, 21).astype(jnp.int32),
        "attn_in": normal_values(splits[7], (3, D, 3 * D), D ** -0.5, 0.1875, ((1, 32),)),
        "attn_out": normal_values(splits[8], (3, D, D), (D // 16) ** -0.5, 0.75, ((1, 32),)),
        "ffn_in": normal_values(splits[9], (2, D, FF), D ** -0.5, 0.1875, ((1, 32),)),
        "ffn_out": normal_values(splits[10], (2, FF, D), FF ** -0.5, 0.09375, ((1, 32),)),
        "embed": draw_embed(jax.random.fold_in(splits[21], 71), 0),
        "down_w": normal_values(splits[12], (2, TASKS, D, A), D ** -0.5, 0.1875, ((2, 32),), jnp.float32),
        "down_m": normal_values(splits[13], (2, TASKS, D, A), (0.0022 * (8 * D * A) ** -0.5), 1.52587890625e-05, ((2, 32),), jnp.float32),
        "down_v": jnp.clip(jnp.exp(math.log(3.814697310203924e-13) - 1.3862944 * jax.random.uniform(splits[14], (2, TASKS, D, A), jnp.float32) ** levels(splits[14], (2, TASKS, D, A), ((2, 32),), -0.2, 0.2)), 9.53674327550981e-14, 3.814697310203924e-13),
        "up_w": normal_values(splits[15], (2, TASKS, A, D), (16 * A) ** -0.5, 0.0625, ((2, 32),), jnp.float32),
        "up_m": normal_values(splits[16], (2, TASKS, A, D), (0.0022 * (8 * D * A) ** -0.5), 1.52587890625e-05, ((2, 32),), jnp.float32),
        "up_v": jnp.clip(jnp.exp(math.log(3.814697310203924e-13) - 1.3862944 * jax.random.uniform(splits[17], (2, TASKS, A, D), jnp.float32) ** levels(splits[17], (2, TASKS, A, D), ((2, 32),), -0.2, 0.2)), 9.53674327550981e-14, 3.814697310203924e-13),
        "norm_params": draw_norm_params(jax.random.fold_in(splits[21], 71), 0),
        "norm_m": normal_values(splits[19], (2, 7, D), (0.0011 * (14 * D) ** -0.5), 0.00012207031, (), jnp.float32),
        "norm_v": jnp.clip(jnp.exp(jax.random.uniform(splits[20], (2, 7, D), jnp.float32, math.log(6.975446262269536e-12), math.log(2.7901785049078143e-11))), 6.975446262269536e-12, 2.7901785049078143e-11),
    }


@jax.custom_vjp
def low(v):
    return lax.optimization_barrier(v.astype(jnp.bfloat16)).astype(jnp.float32)

@jax.custom_vjp
def low_back(v):
    return v

def low_keep(v):
    return (low(v), None)

def low_pass(kept, grad):
    return (grad,)

def back_keep(v):
    return (v, None)

def back_low(kept, grad):
    return (low(grad),)
low.defvjp(low_keep, low_pass)
low_back.defvjp(back_keep, back_low)
norm_epsilon = 1e-05
score_scale = 0.125
clip_limit = 0.02
beta_one = 0.9
beta_two = 0.999
adam_epsilon = 1e-08
rate_adapter = 0.03
rate_norm = 0.25
weight_decay = 0.01
highest = lax.Precision.HIGHEST

def times(left, right):
    return jnp.dot(left, right, precision=highest)

def layer_norm(value, gain, bias):
    centered = value - lax.optimization_barrier(jnp.mean(value, -1, keepdims=True))
    inverse = lax.rsqrt(lax.optimization_barrier(jnp.mean(centered * centered, -1, keepdims=True)) + norm_epsilon)
    return centered * inverse * gain + bias

def attention(query_in, key_in, w_in, w_out, mask):
    width = w_out.shape[0]
    query = low(low_back(times(query_in, w_in[:, :width])))
    pair = low(low_back(times(key_in, w_in[:, width:])))
    heads_query = query.reshape(query.shape[0], -1, HDIM)
    keys = pair[:, :width].reshape(pair.shape[0], -1, HDIM)
    values = pair[:, width:].reshape(pair.shape[0], -1, HDIM)
    raw = jnp.einsum('qhd,khd->hqk', heads_query, keys, precision=highest) * score_scale
    scores = low_back(jnp.where(mask[None], raw, -1000000000.0))
    probs = low(jax.nn.softmax(scores, -1))
    out = jnp.einsum('hqk,khd->qhd', probs, values, precision=highest).reshape(query.shape[0], width)
    return low_back(times(low(low_back(out)), w_out))

def feed(value, w_first, w_second, down, upward):
    low_in = low(value)
    hidden = low_back(times(low_in, w_first))
    branch = low_back(times(low(jax.nn.gelu(hidden, approximate=False)), w_second))
    inner = low_back(times(low_in, down))
    adapter = low_back(times(low(jax.nn.gelu(inner, approximate=False)), upward))
    return branch + 4.0 * adapter

def adam_update(weight, first, second, grad, rate, decay, count_step):
    first_new = beta_one * first + (1.0 - beta_one) * grad
    second_new = beta_two * second + (1.0 - beta_two) * grad * grad
    first_hat = first_new / (1.0 - jnp.power(beta_one, count_step))
    second_hat = second_new / (1.0 - jnp.power(beta_two, count_step))
    weight_new = weight - rate * (first_hat / (jnp.sqrt(second_hat) + adam_epsilon) + decay * weight)
    return (weight_new, first_new, second_new)

def reference(src_embed, tgt_embed, targets, src_len, tgt_len, task, step, attn_in, attn_out, ffn_in, ffn_out, embed, down_w, down_m, down_v, up_w, up_m, up_v, norm_params, norm_m, norm_v):
    items = MICRO * GROUPS
    sources = src_embed.astype(jnp.float32).reshape(items, SRC, D)
    targets_in = tgt_embed.astype(jnp.float32).reshape(items, TGT, D)
    target_ids = targets.reshape(items, TGT).astype(jnp.int32)
    src_lengths = src_len.reshape(items).astype(jnp.int32)
    tgt_lengths = tgt_len.reshape(items).astype(jnp.int32)
    kinds = task.reshape(items).astype(jnp.int32)
    attn_all = attn_in.astype(jnp.float32)
    out_all = attn_out.astype(jnp.float32)
    first_all = ffn_in.astype(jnp.float32)
    second_all = ffn_out.astype(jnp.float32)
    table = embed.astype(jnp.float32)
    count = jnp.sum(tgt_len).astype(jnp.float32)
    src_pos = jnp.arange(SRC, dtype=jnp.int32)
    tgt_pos = jnp.arange(TGT, dtype=jnp.int32)

    def loss_fn(down_param, up_param, norms):
        down_low = low(down_param)
        up_low = low(up_param)

        def one_item(source, target_in, target_id, slen, tlen, kind):

            def norm_at(value, index):
                return layer_norm(value, norms[0, index], norms[1, index])
            enc_mask = jnp.broadcast_to(src_pos[None, :] < slen, (SRC, SRC))
            x0 = norm_at(source, 0)
            x0_low = low(x0)
            x1 = norm_at(x0 + attention(x0_low, x0_low, attn_all[0], out_all[0], enc_mask), 1)
            x2 = norm_at(x1 + feed(x1, first_all[0], second_all[0], down_low[0, kind], up_low[0, kind]), 2)
            self_mask = (tgt_pos[None, :] <= tgt_pos[:, None]) & (tgt_pos[None, :] < tlen)
            cross_mask = jnp.broadcast_to(src_pos[None, :] < slen, (TGT, SRC))
            y0 = norm_at(target_in, 3)
            y0_low = low(y0)
            y1 = norm_at(y0 + attention(y0_low, y0_low, attn_all[1], out_all[1], self_mask), 4)
            y2 = norm_at(y1 + attention(low(y1), low(x2), attn_all[2], out_all[2], cross_mask), 5)
            y3 = norm_at(y2 + feed(y2, first_all[1], second_all[1], down_low[1, kind], up_low[1, kind]), 6)
            logits = low_back(times(low(y3), table.T))
            logsum = jax.nn.logsumexp(logits, -1)
            picked = jnp.take_along_axis(logits, target_id[:, None], 1)[:, 0]
            row_loss = logsum - 0.9 * picked - 0.1 * lax.optimization_barrier(jnp.mean(logits, -1))
            return jnp.sum(jnp.where(tgt_pos < tlen, row_loss, 0.0))
        checked = jax.checkpoint(one_item)

        def scan_step(carry, inputs):
            return (carry + checked(*inputs), None)
        total, unused = lax.scan(scan_step, jnp.zeros((), jnp.float32), (sources, targets_in, target_ids, src_lengths, tgt_lengths, kinds))
        return (total / count, total)
    loss, pullback, loss_sum = jax.vjp(loss_fn, down_w, up_w, norm_params, has_aux=True)
    down_grad, up_grad, norm_raw = pullback(jnp.ones((), jnp.float32))
    grad_norm = jnp.sqrt(jnp.sum(down_grad * down_grad) + jnp.sum(up_grad * up_grad) + jnp.sum(norm_raw * norm_raw))
    factor = clip_limit / jnp.maximum(grad_norm, clip_limit)
    count_step = step[0].astype(jnp.float32)
    down_new = adam_update(down_w, down_m, down_v, factor * down_grad, rate_adapter, weight_decay, count_step)
    up_new = adam_update(up_w, up_m, up_v, factor * up_grad, rate_adapter, weight_decay, count_step)
    norm_grad = factor * norm_raw
    norm_new = adam_update(norm_params, norm_m, norm_v, norm_grad, rate_norm, 0.0, count_step)
    return (loss_sum, count, grad_norm, down_new[0], down_new[1], down_new[2], up_new[0], up_new[1], up_new[2], norm_new[0], norm_new[1], norm_new[2], norm_grad)
```

```python
import functools

import jax
import jax.numpy as jnp
from jax import lax
from jax.experimental import pallas as pl
from jax.experimental.pallas import tpu as pltpu
from jax.sharding import PartitionSpec as P

HDIM = 64


norm_epsilon = 1e-05
score_scale = 0.125
clip_limit = 0.02
beta_one = 0.9
beta_two = 0.999
adam_epsilon = 1e-08
rate_adapter = 0.03
rate_norm = 0.25
weight_decay = 0.01


def bfloat(value):
    return value.astype(jnp.bfloat16)


def times_plain(left, right):
    return jnp.dot(left, right, preferred_element_type=jnp.float32)


def times_first(left, right):
    return lax.dot_general(
        left, right, (((0,), (0,)), ((), ())), preferred_element_type=jnp.float32
    )


def times_second(left, right):
    return lax.dot_general(
        left, right, (((1,), (1,)), ((), ())), preferred_element_type=jnp.float32
    )


def norm_forward(value, gain, bias):
    centered = value - jnp.mean(value, -1, keepdims=True)
    inverse = lax.rsqrt(jnp.mean(centered * centered, -1, keepdims=True) + norm_epsilon)
    normed = centered * inverse
    return (normed * gain + bias, (normed, inverse))


def norm_backward(grad, cache, gain):
    normed, inverse = cache
    scaled = grad * gain
    value_grad = inverse * (
        scaled
        - jnp.mean(scaled, -1, keepdims=True)
        - normed * jnp.mean(scaled * normed, -1, keepdims=True)
    )
    return (value_grad, jnp.stack([jnp.sum(grad * normed, 0), jnp.sum(grad, 0)]))


def gelu_slope(value):
    return (
        0.5 * (1.0 + lax.erf(value * 0.7071067811865476))
        + value * jnp.exp(-0.5 * value * value) * 0.3989422804014327
    )


def split_heads(value):
    return value.reshape(value.shape[0], -1, HDIM)


AXES = ("seq", "kv")
MEBI = 2**20
LOWEST = -3e38


def swap(value, seq_mask, kv_mask):
    seq_count, kv_count = lax.axis_size("seq"), lax.axis_size("kv")
    pairs = [
        (s * kv_count + z, (s ^ seq_mask) * kv_count + (z ^ kv_mask))
        for s in range(seq_count)
        for z in range(kv_count)
    ]
    return lax.ppermute(value, AXES, pairs)


def plane_bits():
    count = lax.axis_size("seq").bit_length() - 2
    bits = [2 << place for place in range(count)]
    return (bits[: count // 2], bits[count // 2 :])


def after(value, earlier):
    return lax.optimization_barrier((value, earlier))[0]


def spread(blocks, bits):
    for bit in bits:
        keys = sorted(blocks)
        got = swap(jnp.stack([blocks[key] for key in keys]), bit, 0)
        blocks = blocks | {key | bit: got[place] for place, key in enumerate(keys)}
    return blocks


def gather_depth_first(own, earlier):
    own = after(own, earlier) if earlier is not None else own
    kv_count = lax.axis_size("kv")
    column = [own] + [swap(own, 0, step) for step in range(1, kv_count)]
    half = kv_count // 2
    x_bits, y_bits = plane_bits()
    pieces = []
    for first, bits in ((0, x_bits + y_bits), (half, y_bits + x_bits)):
        parts = [((0,), jnp.stack(column[first : first + half]))]
        stack = parts[0][1][None]
        labels = [0]
        for bit in bits:
            got = swap(stack, bit, 0)
            pieces.append((labels, first, stack)) if bit == bits[-1] else None
            fresh = [label | bit for label in labels]
            if bit == bits[-1]:
                pieces.append((fresh, first, got))
            else:
                stack = jnp.concatenate([stack, got])
                labels = labels + fresh
    pieces = pieces + [
        ([label | 1 for label in labels], first, swap(stack, 1, 0))
        for labels, first, stack in pieces
    ]
    return pieces, column[-1]


def gather_plane_first(own, earlier):
    kv_count = lax.axis_size("kv")
    x_bits, y_bits = plane_bits()
    half = own.shape[1] // 2
    stacks = []
    for part, bits in ((own[:, :half], x_bits + y_bits), (own[:, half:], y_bits + x_bits)):
        blocks = spread({0: part}, bits)
        labels = sorted(blocks)
        stacks.append(jnp.stack([blocks[label] for label in labels]))
    whole = jnp.concatenate(stacks, 2)
    sent = after(whole, earlier)
    pieces = [(labels, 0, whole[:, None])] + [
        (labels, step, swap(sent, 0, step)[:, None]) for step in range(1, kv_count)
    ]
    pieces = pieces + [
        ([label | 1 for label in names], first, swap(stack, 1, 0))
        for names, first, stack in pieces
    ]
    return pieces


def place_kernel(plan, where_ref, *refs):
    sources = refs[: len(plan)]
    count = len(refs) - len(plan) - 1
    targets = refs[len(plan) : len(plan) + count]
    sems = refs[-1]
    own = where_ref[0]
    kind = where_ref[1]
    copies = []
    for source, labels in zip(sources, plan):
        for first, row in enumerate(labels):
            for second, label in enumerate(row):
                block = source.at[first, second]
                where = own ^ label
                if count == 2 and len(source.shape) == 5:
                    start = 0
                    for target in targets:
                        width = target.shape[-1]
                        copies.append((block.at[0, :, start : start + width], target.at[where]))
                        start += width
                elif count == 1:
                    copies.append((block.at[0], targets[0].at[where]))
                else:
                    for layer in range(2):
                        copies.append((block.at[2 * layer + kind], targets[0].at[layer, where]))
                        copies.append((block.at[4 + 2 * layer + kind], targets[1].at[layer, :, where]))
    started = []
    for place, (origin, target) in enumerate(copies):
        copy = pltpu.make_async_copy(origin, target, sems.at[place])
        copy.start()
        started.append(copy)
    for copy in started:
        copy.wait()


def place_blocks(pieces, where, shapes):
    kv_count = lax.axis_size("kv")
    plan = []
    total = 0
    for labels, first, stack in pieces:
        plan.append([[label * kv_count + first + k for k in range(stack.shape[1])] for label in labels])
        total += len(labels) * stack.shape[1]
    copies = total * (4 if pieces[0][2].ndim == 6 else len(shapes))
    anywhere = pl.BlockSpec(memory_space=pl.ANY)
    return pl.pallas_call(
        functools.partial(place_kernel, plan),
        grid_spec=pltpu.PrefetchScalarGridSpec(
            num_scalar_prefetch=1,
            grid=(1,),
            in_specs=[anywhere] * len(pieces),
            out_specs=[anywhere] * len(shapes),
            scratch_shapes=[pltpu.SemaphoreType.DMA((copies,))],
        ),
        out_shape=[jax.ShapeDtypeStruct(shape, jnp.bfloat16) for shape in shapes],
    )(where, *[stack for _, _, stack in pieces])


def with_partner(value):
    return jnp.concatenate([value, swap(value, 1, 0)])


def scores_of(query, keys, mask):
    raw = (
        jnp.einsum(
            "qhd,khd->hqk",
            split_heads(query),
            split_heads(keys),
            preferred_element_type=jnp.float32,
        )
        * score_scale
    )
    return jnp.where(mask[None], raw, -1000000000.0)


def attention_forward(query_in, key_in, w_in, w_out, mask):
    width = w_out.shape[0]
    query = bfloat(times_plain(query_in, w_in[:, :width]))
    gathered = with_partner(bfloat(times_plain(key_in, w_in[:, width:])))
    scores = scores_of(query, gathered[:, :width], mask)
    top = jnp.max(scores, -1, keepdims=True)
    logsum = top + jnp.log(jnp.sum(jnp.exp(scores - top), -1, keepdims=True))
    weights = bfloat(jnp.exp(scores - logsum))
    out = jnp.einsum(
        "hqk,khd->qhd",
        weights,
        split_heads(gathered[:, width:]),
        preferred_element_type=jnp.float32,
    )
    out_low = bfloat(out.reshape(query.shape[0], width))
    return (times_plain(out_low, w_out), (query, gathered, logsum))


def attention_backward(branch_grad, cache, w_in, w_out, mask):
    query, gathered, logsum = cache
    width = w_out.shape[0]
    keys = gathered[:, :width]
    out_grad = split_heads(bfloat(times_second(bfloat(branch_grad), w_out)))
    probs = jnp.exp(scores_of(query, keys, mask) - logsum)
    value_grad = jnp.einsum(
        "hqk,qhd->khd", bfloat(probs), out_grad, preferred_element_type=jnp.float32
    )
    prob_grad = jnp.einsum(
        "qhd,khd->hqk",
        out_grad,
        split_heads(gathered[:, width:]),
        preferred_element_type=jnp.float32,
    )
    score_grad = bfloat(probs * (prob_grad - jnp.sum(probs * prob_grad, -1, keepdims=True)))
    query_grad = (
        jnp.einsum(
            "hqk,khd->qhd", score_grad, split_heads(keys), preferred_element_type=jnp.float32
        )
        * score_scale
    )
    key_grad = (
        jnp.einsum(
            "hqk,qhd->khd", score_grad, split_heads(query), preferred_element_type=jnp.float32
        )
        * score_scale
    )
    stacked = jnp.concatenate(
        [key_grad.reshape(keys.shape[0], width), value_grad.reshape(keys.shape[0], width)], 1
    )
    rows = keys.shape[0] // 2
    pair_grad = stacked[:rows] + swap(bfloat(stacked[rows:]), 1, 0).astype(jnp.float32)
    query_in_grad = times_second(bfloat(query_grad.reshape(query.shape[0], width)), w_in[:, :width])
    key_in_grad = times_second(bfloat(pair_grad), w_in[:, width:])
    return (query_in_grad, key_in_grad)


def feed_forward(value, w_first, w_second, down, upward):
    low_in = bfloat(value)
    hidden = times_plain(low_in, w_first)
    branch = times_plain(bfloat(jax.nn.gelu(hidden, approximate=False)), w_second)
    inner = times_plain(low_in, down)
    inner_low = bfloat(jax.nn.gelu(inner, approximate=False))
    return (branch + 4.0 * times_plain(inner_low, upward), (low_in, hidden, inner, inner_low))


def feed_backward(grad, cache, w_first, w_second, down, upward):
    low_in, hidden, inner, inner_low = cache
    hidden_grad = bfloat(times_second(bfloat(grad), w_second) * gelu_slope(hidden))
    adapter_grad = bfloat(4.0 * grad)
    upward_grad = times_first(inner_low, adapter_grad)
    inner_grad = bfloat(times_second(adapter_grad, upward) * gelu_slope(inner))
    down_grad = times_first(low_in, inner_grad)
    value_grad = times_second(hidden_grad, w_first) + times_second(inner_grad, down)
    return (value_grad, down_grad, upward_grad)


def vocab_kernel(count, tile, rows_ref, table_ref, mixed_ref, stats_ref, scores):
    rows = rows_ref[...]
    block = rows.shape[0]
    padded = table_ref.shape[0]
    top = jnp.full((block, 1), LOWEST, jnp.float32)
    for start in range(0, padded, tile):
        part = times_second(rows, table_ref[start : start + tile, :])
        if start + tile > count:
            entry = lax.broadcasted_iota(jnp.int32, part.shape, 1) + start
            part = jnp.where(entry < count, part, LOWEST)
        scores[:, start : start + tile] = part
        top = jnp.maximum(top, jnp.max(part, 1, keepdims=True))
    total = jnp.zeros((block, 1), jnp.float32)
    mixed = jnp.zeros(mixed_ref.shape, jnp.float32)
    for start in range(0, padded, tile):
        weights = jnp.exp(scores[:, start : start + tile] - top)
        total = total + jnp.sum(weights, 1, keepdims=True)
        mixed = mixed + times_plain(bfloat(weights), table_ref[start : start + tile, :])
    mixed_ref[...] = mixed
    stats_ref[...] = jnp.concatenate(
        [jnp.broadcast_to(top, (block, 64)), jnp.broadcast_to(total, (block, 64))], 1
    )


def vocab_pass(rows, table, count, block, tile):
    total, width = rows.shape
    padded = table.shape[0]
    return pl.pallas_call(
        functools.partial(vocab_kernel, count, tile),
        grid=(total // block,),
        in_specs=[
            pl.BlockSpec((block, width), lambda i: (i, 0)),
            pl.BlockSpec((padded, width), lambda i: (0, 0), pipeline_mode=pl.Buffered(1)),
        ],
        out_specs=[
            pl.BlockSpec((block, width), lambda i: (i, 0)),
            pl.BlockSpec((block, 128), lambda i: (i, 0)),
        ],
        out_shape=[
            jax.ShapeDtypeStruct((total, width), jnp.float32),
            jax.ShapeDtypeStruct((total, 128), jnp.float32),
        ],
        scratch_shapes=[pltpu.VMEM((block, padded), jnp.float32)],
        compiler_params=pltpu.CompilerParams(vmem_limit_bytes=56 * MEBI),
        cost_estimate=pl.CostEstimate(
            flops=4 * total * width * padded,
            bytes_accessed=2 * padded * width + 6 * total * width,
            transcendentals=total * padded,
        ),
    )(rows, table)


def halved_sum(blocks, bits):
    for bit in bits:
        keys = [key for key in sorted(blocks) if not key & bit]
        got = swap(jnp.stack([bfloat(blocks[key | bit]) for key in keys]), bit, 0)
        blocks = {key: blocks[key] + got[place].astype(jnp.float32) for place, key in enumerate(keys)}
    return blocks


def pick(value, axis, index):
    return lax.dynamic_index_in_dim(value, index, axis, keepdims=False)


def adapter_sum(down_grad, up_grad, kind, tasks):
    seq_count, kv_count = lax.axis_size("seq"), lax.axis_size("kv")
    seq_index, kv_index = lax.axis_index("seq"), lax.axis_index("kv")
    devices = seq_count * kv_count
    hidden = down_grad.shape[1]
    down_rows = down_grad.shape[0] // devices
    up_rows = up_grad.shape[0] // devices
    folds = up_grad.shape[1] // hidden
    down_part = down_grad.reshape(devices, down_rows, hidden)
    up_part = (
        up_grad.reshape(devices, up_rows, folds, hidden)
        .transpose(0, 2, 1, 3)
        .reshape(devices, folds * up_rows, hidden)
    )
    grad = jnp.concatenate([down_part, up_part], 1)
    height = grad.shape[1]
    core = seq_index % 2
    grad = grad.reshape(seq_count // 2, 2, kv_count, height, hidden)
    grad = pick(grad, 1, core) + swap(bfloat(pick(grad, 1, 1 - core)), 1, 0).astype(jnp.float32)
    x_bits, y_bits = plane_bits()
    by_task = []
    for task in range(tasks):
        part = grad * (kind == task).astype(jnp.float32)
        part = part.reshape([2] * (len(x_bits) + len(y_bits)) + [kv_count, height, hidden])
        order = (x_bits + y_bits, y_bits + x_bits)[task % 2]
        left = [bit for bit in reversed(x_bits + y_bits)]
        for bit in order:
            axis = left.index(bit)
            left.remove(bit)
            mine = (seq_index // bit) % 2
            part = pick(part, axis, mine) + swap(bfloat(pick(part, axis, 1 - mine)), bit, 0).astype(
                jnp.float32
            )
        by_task.append(part)
    part = jnp.stack(by_task, 1)
    total = pick(part, 0, kv_index)
    for step in range(1, kv_count):
        sent = bfloat(pick(part, 0, kv_index ^ step))
        total = total + swap(sent, 0, step).astype(jnp.float32)
    down_total = total[:, :down_rows]
    up_total = (
        total[:, down_rows:]
        .reshape(tasks, folds, up_rows, hidden)
        .transpose(0, 2, 1, 3)
        .reshape(tasks, up_rows, folds * hidden)
    )
    return (down_total, up_total)


def total_sum(value):
    step = 1
    while step < lax.axis_size("seq"):
        value = value + swap(value, step, 0)
        step *= 2
    step = 1
    while step < lax.axis_size("kv"):
        value = value + swap(value, 0, step)
        step *= 2
    return value


def item_rows(embeds):
    seq_count, kv_count = lax.axis_size("seq"), lax.axis_size("kv")
    kv_index = lax.axis_index("kv")
    got = []
    for turn in range(2):
        pairs = []
        for s in range(seq_count):
            for z in range(kv_count):
                source = (s - s % 2 + z % 2) * kv_count + 2 * (s % 2) + ((z // 2) ^ turn)
                pairs.append((source, s * kv_count + z))
        sent = pick(embeds[:, 0], 0, (kv_index % 2) ^ turn)
        got.append(lax.ppermute(sent, AXES, pairs))
    swapped = kv_index // 2 == 1
    return jnp.concatenate(
        [jnp.where(swapped, got[1], got[0]), jnp.where(swapped, got[0], got[1])]
    )


def adam_update(weight, first, second, grad, rate, decay, count_step):
    first_new = beta_one * first + (1.0 - beta_one) * grad
    second_new = beta_two * second + (1.0 - beta_two) * grad * grad
    first_hat = first_new / (1.0 - jnp.power(beta_one, count_step))
    second_hat = second_new / (1.0 - jnp.power(beta_two, count_step))
    weight_new = weight - rate * (
        first_hat / (jnp.sqrt(second_hat) + adam_epsilon) + decay * weight
    )
    return (weight_new, first_new, second_new)


def per_device(
    src_embed,
    tgt_embed,
    targets,
    src_len,
    tgt_len,
    task,
    step,
    attn_in,
    attn_out,
    ffn_in,
    ffn_out,
    embed,
    down_w,
    down_m,
    down_v,
    up_w,
    up_m,
    up_v,
    norm_params,
    norm_m,
    norm_v,
):
    seq_count, kv_count = lax.axis_size("seq"), lax.axis_size("kv")
    seq_index, kv_index = lax.axis_index("seq"), lax.axis_index("kv")
    devices = seq_count * kv_count
    width = attn_out.shape[2]
    hidden = ffn_in.shape[2]
    bottleneck = down_w.shape[3]
    tasks = down_w.shape[1]
    vocab_rows = embed.shape[0]
    vocab_total = vocab_rows * seq_count
    core = seq_index % 2
    batch = kv_index // 2
    item = seq_index - core + kv_index % 2
    source_length = src_len[batch, item]
    target_length = tgt_len[batch, item]
    kind = task[batch, item]
    count = jnp.sum(tgt_len).astype(jnp.float32)
    gains = norm_params[0]
    biases = norm_params[1]

    source = item_rows(src_embed)
    target = item_rows(tgt_embed)
    enc_rows = source.shape[0]
    dec_rows = target.shape[0]
    ids_all = lax.all_gather(targets, "kv", axis=2, tiled=True)

    share = width // devices
    up_low = bfloat(up_w).reshape(2 * tasks, up_w.shape[2], 2, bottleneck).transpose(0, 2, 1, 3)
    down_low = bfloat(down_w).reshape(2 * tasks, 2, share // 2, bottleneck)
    own = [
        jnp.concatenate([attn_in[0], attn_out[0]], 1)[None],
        jnp.concatenate([attn_in[1], attn_out[1]], 1)[None],
        ffn_in[0][None],
        jnp.concatenate([down_low, up_low]),
        ffn_out[0][None],
        jnp.concatenate([attn_in[2], attn_out[2]], 1)[None],
        ffn_in[1][None],
        ffn_out[1][None],
    ]
    attn_shapes = [(devices, share, 3 * width), (devices, share, width)]
    first_shapes = [(devices, share, hidden)]
    second_shapes = [(devices, hidden // devices, width)]
    adapter_shapes = [
        (2, devices, 2, share // 2, bottleneck),
        (2, 2, devices, up_w.shape[2], bottleneck),
    ]
    shapes = [
        attn_shapes,
        attn_shapes,
        first_shapes,
        adapter_shapes,
        second_shapes,
        attn_shapes,
        first_shapes,
        second_shapes,
    ]
    where = jnp.stack([seq_index * kv_count + kv_index, kind]).astype(jnp.int32)
    placed = []
    earlier = source
    for block, shape in zip(own[:-1], shapes[:-1]):
        pieces, earlier = gather_depth_first(block, earlier)
        placed.append(place_blocks(pieces, where, shape))
    placed.append(place_blocks(gather_plane_first(own[-1], earlier), where, shapes[-1]))
    attn_w = [
        (placed[g][0].reshape(width, 3 * width), placed[g][1].reshape(width, width))
        for g in (0, 1, 5)
    ]
    first_w = [placed[g][0].reshape(width, hidden) for g in (2, 6)]
    second_w = [placed[g][0].reshape(hidden, width) for g in (4, 7)]
    down_all = placed[3][0].reshape(2, width, bottleneck)
    up_all = placed[3][1].reshape(2, 2, bottleneck, bottleneck)
    up_all = jnp.concatenate([up_all[:, 0], up_all[:, 1]], 2)

    half = dec_rows // 2
    relative = seq_index ^ jnp.arange(seq_count, dtype=jnp.int32)
    row_items = relative - relative % 2 + kv_index % 2
    row_pos = (
        (relative % 2)[None, :, None] * dec_rows
        + jnp.arange(2, dtype=jnp.int32)[:, None, None] * half
        + jnp.arange(half, dtype=jnp.int32)[None, None, :]
    )
    plane_ids = pick(ids_all, 0, batch)
    row_ids = plane_ids[row_items[None, :, None], row_pos].reshape(-1)
    plane_lengths = pick(tgt_len, 0, batch)[row_items]
    alive = (row_pos < plane_lengths[None, :, None]).reshape(-1).astype(jnp.float32)
    live = alive / count
    local_ids = row_ids - seq_index * vocab_rows
    local_hit = (local_ids >= 0) & (local_ids < vocab_rows)
    target_rows = jnp.take(embed, jnp.clip(local_ids, 0, vocab_rows - 1), axis=0)
    target_rows = jnp.where(local_hit[:, None], target_rows, jnp.zeros((), jnp.bfloat16))
    table_sum = jnp.sum(embed.astype(jnp.float32), 0)
    tile = 1280
    table = jnp.pad(embed, ((0, -vocab_rows % tile), (0, 0)))

    enc_order = jnp.stack([core, 1 - core])[:, None] * enc_rows + jnp.arange(enc_rows)[None]
    dec_order = jnp.stack([core, 1 - core])[:, None] * dec_rows + jnp.arange(dec_rows)[None]
    src_keys = enc_order.reshape(-1)
    dec_keys = dec_order.reshape(-1)
    dec_query = core * dec_rows + jnp.arange(dec_rows)
    enc_mask = jnp.broadcast_to(src_keys[None, :] < source_length, (enc_rows, src_keys.shape[0]))
    self_mask = (dec_keys[None, :] <= dec_query[:, None]) & (dec_keys[None, :] < target_length)
    cross_mask = jnp.broadcast_to(src_keys[None, :] < source_length, (dec_rows, src_keys.shape[0]))

    x0, cache0 = norm_forward(source.astype(jnp.float32), gains[0], biases[0])
    x0_low = bfloat(x0)
    branch, enc_attn = attention_forward(x0_low, x0_low, *attn_w[0], enc_mask)
    x1, cache1 = norm_forward(x0 + branch, gains[1], biases[1])
    branch, enc_feed = feed_forward(x1, first_w[0], second_w[0], down_all[0], up_all[0])
    x2, cache2 = norm_forward(x1 + branch, gains[2], biases[2])
    y0, cache3 = norm_forward(target.astype(jnp.float32), gains[3], biases[3])
    y0_low = bfloat(y0)
    branch, self_attn = attention_forward(y0_low, y0_low, *attn_w[1], self_mask)
    y1, cache4 = norm_forward(y0 + branch, gains[4], biases[4])
    branch, cross_attn = attention_forward(bfloat(y1), bfloat(x2), *attn_w[2], cross_mask)
    y2, cache5 = norm_forward(y1 + branch, gains[5], biases[5])
    branch, dec_feed = feed_forward(y2, first_w[1], second_w[1], down_all[1], up_all[1])
    y3, cache6 = norm_forward(y2 + branch, gains[6], biases[6])

    x_bits, y_bits = plane_bits()
    orders = ([1] + x_bits + y_bits, [1] + y_bits + x_bits)
    y3_low = bfloat(y3)
    gathered = []
    for part, bits in zip((y3_low[:half], y3_low[half:]), orders):
        blocks = spread({0: part}, bits)
        gathered += [blocks[key] for key in sorted(blocks)]
    rows = jnp.concatenate(gathered)
    mixed, stats = vocab_pass(rows, table, vocab_rows, 512, tile)
    top = stats[:, 0].reshape(2, seq_count, half)
    total = stats[:, 64].reshape(2, seq_count, half)
    row_top, row_total = top, total
    for bit in [1] + x_bits + y_bits:
        flipped = [key ^ bit for key in range(seq_count)]
        got = swap(jnp.stack([row_top, row_total]), bit, 0)
        got = jnp.stack([got[:, :, key] for key in flipped], 2)
        best = jnp.maximum(row_top, got[0])
        row_total = row_total * jnp.exp(row_top - best) + got[1] * jnp.exp(got[0] - best)
        row_top = best
    logsum = (row_top + jnp.log(row_total)).reshape(-1)
    own_rows = (jnp.arange(seq_count) == 0).astype(jnp.float32)
    own_rows = jnp.broadcast_to(own_rows[None, :, None], row_top.shape).reshape(-1)
    linear = 0.9 * target_rows.astype(jnp.float32) + (0.1 / vocab_total) * table_sum[None]
    loss_part = jnp.sum(alive * own_rows * logsum) - jnp.sum(
        alive[:, None] * rows.astype(jnp.float32) * linear
    )
    row_scale = jnp.exp(top.reshape(-1) - logsum)
    share_grad = (mixed * row_scale[:, None] - linear) * live[:, None]
    share_grad = share_grad.reshape(2, seq_count, half, width)
    final_grad = jnp.concatenate(
        [
            halved_sum({key: share_grad[h, key] for key in range(seq_count)}, orders[h])[0]
            for h in range(2)
        ]
    )

    grad, grad6 = norm_backward(final_grad, cache6, gains[6])
    inner_grad, down_grad, up_grad = feed_backward(
        grad, dec_feed, first_w[1], second_w[1], down_all[1], up_all[1]
    )
    dec_sums = adapter_sum(down_grad, up_grad, kind, tasks)
    grad, grad5 = norm_backward(grad + inner_grad, cache5, gains[5])
    query_grad, enc_grad = attention_backward(grad, cross_attn, *attn_w[2], cross_mask)
    dec_grad, grad4 = norm_backward(grad + query_grad, cache4, gains[4])
    grad, grad2 = norm_backward(enc_grad, cache2, gains[2])
    inner_grad, down_grad, up_grad = feed_backward(
        grad, enc_feed, first_w[0], second_w[0], down_all[0], up_all[0]
    )
    enc_sums = adapter_sum(down_grad, up_grad, kind, tasks)
    query_grad, key_grad = attention_backward(dec_grad, self_attn, *attn_w[1], self_mask)
    _, grad3 = norm_backward(dec_grad + query_grad + key_grad, cache3, gains[3])
    grad, grad1 = norm_backward(grad + inner_grad, cache1, gains[1])
    query_grad, key_grad = attention_backward(grad, enc_attn, *attn_w[0], enc_mask)
    _, grad0 = norm_backward(grad + query_grad + key_grad, cache0, gains[0])

    norm_grad = jnp.stack([grad0, grad1, grad2, grad3, grad4, grad5, grad6], 1)
    down_part = jnp.stack([enc_sums[0], dec_sums[0]])
    up_part = jnp.stack([enc_sums[1], dec_sums[1]])
    square = jnp.sum(down_part * down_part) + jnp.sum(up_part * up_part)
    scalars = jnp.zeros((1, width), jnp.float32).at[0, 0].set(loss_part).at[0, 1].set(square)
    summed = total_sum(jnp.concatenate([norm_grad.reshape(-1, width), scalars]))
    norm_sum = summed[:-1].reshape(norm_grad.shape)
    loss_sum = summed[-1, 0]
    grad_norm = jnp.sqrt(summed[-1, 1] + jnp.sum(norm_sum * norm_sum))
    factor = clip_limit / jnp.maximum(grad_norm, clip_limit)
    count_step = step[0].astype(jnp.float32)
    down_new = adam_update(
        down_w, down_m, down_v, factor * down_part, rate_adapter, weight_decay, count_step
    )
    up_new = adam_update(up_w, up_m, up_v, factor * up_part, rate_adapter, weight_decay, count_step)
    norm_grad_out = factor * norm_sum
    norm_new = adam_update(norm_params, norm_m, norm_v, norm_grad_out, rate_norm, 0.0, count_step)
    return (
        loss_sum,
        count,
        grad_norm,
        down_new[0],
        down_new[1],
        down_new[2],
        up_new[0],
        up_new[1],
        up_new[2],
        norm_new[0],
        norm_new[1],
        norm_new[2],
        norm_grad_out,
    )


def solution(mesh):
    placed = (
        P(None, "seq", "kv", None),
        P(None, "seq", "kv", None),
        P(None, None, "kv"),
        P(),
        P(),
        P(),
        P(),
        P(None, ("seq", "kv"), None),
        P(None, ("seq", "kv"), None),
        P(None, ("seq", "kv"), None),
        P(None, ("seq", "kv"), None),
        P("seq", None),
        P(None, None, ("seq", "kv"), None),
        P(None, None, ("seq", "kv"), None),
        P(None, None, ("seq", "kv"), None),
        P(None, None, ("seq", "kv"), None),
        P(None, None, ("seq", "kv"), None),
        P(None, None, ("seq", "kv"), None),
        P(),
        P(),
        P(),
    )
    return jax.shard_map(
        per_device,
        mesh=mesh,
        in_specs=placed,
        out_specs=(
            P(),
            P(),
            P(),
            P(None, None, ("seq", "kv"), None),
            P(None, None, ("seq", "kv"), None),
            P(None, None, ("seq", "kv"), None),
            P(None, None, ("seq", "kv"), None),
            P(None, None, ("seq", "kv"), None),
            P(None, None, ("seq", "kv"), None),
            P(),
            P(),
            P(),
            P(),
        ),
        check_vma=False,
    )
```

```python
import functools

import jax
import jax.numpy as jnp
from jax import lax
from jax.experimental import pallas as pl
from jax.experimental.pallas import tpu as pltpu
from jax.sharding import PartitionSpec as P

HDIM = 64


norm_epsilon = 1e-05
score_scale = 0.125
clip_limit = 0.02
beta_one = 0.9
beta_two = 0.999
adam_epsilon = 1e-08
rate_adapter = 0.03
rate_norm = 0.25
weight_decay = 0.01


def bfloat(value):
    return value.astype(jnp.bfloat16)


def times_plain(left, right):
    return jnp.dot(left, right, preferred_element_type=jnp.float32)


def times_first(left, right):
    return lax.dot_general(
        left, right, (((0,), (0,)), ((), ())), preferred_element_type=jnp.float32
    )


def times_second(left, right):
    return lax.dot_general(
        left, right, (((1,), (1,)), ((), ())), preferred_element_type=jnp.float32
    )


def norm_forward(value, gain, bias):
    centered = value - jnp.mean(value, -1, keepdims=True)
    inverse = lax.rsqrt(jnp.mean(centered * centered, -1, keepdims=True) + norm_epsilon)
    normed = centered * inverse
    return (normed * gain + bias, (normed, inverse))


def norm_backward(grad, cache, gain):
    normed, inverse = cache
    scaled = grad * gain
    value_grad = inverse * (
        scaled
        - jnp.mean(scaled, -1, keepdims=True)
        - normed * jnp.mean(scaled * normed, -1, keepdims=True)
    )
    return (value_grad, jnp.stack([jnp.sum(grad * normed, 0), jnp.sum(grad, 0)]))


def gelu_slope(value):
    return (
        0.5 * (1.0 + lax.erf(value * 0.7071067811865476))
        + value * jnp.exp(-0.5 * value * value) * 0.3989422804014327
    )


AXES = ("seq", "kv")
MEBI = 2**20
LOWEST = -3e38
LIVE_ROWS = 64
LIGHT = pl.CostEstimate(flops=1, bytes_accessed=1, transcendentals=0)


def swap(value, seq_mask, kv_mask):
    seq_count, kv_count = lax.axis_size("seq"), lax.axis_size("kv")
    pairs = [
        (s * kv_count + z, (s ^ seq_mask) * kv_count + (z ^ kv_mask))
        for s in range(seq_count)
        for z in range(kv_count)
    ]
    return lax.ppermute(value, AXES, pairs)


def trade_bits(value):
    seq_count, kv_count = lax.axis_size("seq"), lax.axis_size("kv")
    pairs = [
        (s * kv_count + z, (s - s % 4 + 2 * (s % 2) + s // 2 % 2) * kv_count + z)
        for s in range(seq_count)
        for z in range(kv_count)
    ]
    return lax.ppermute(value, AXES, pairs)


def plane_bits():
    count = lax.axis_size("seq").bit_length() - 2
    bits = [2 << place for place in range(count)]
    return (bits[: count // 2], bits[count // 2 :])


def after(value, earlier):
    return lax.optimization_barrier((value, earlier))[0]


def pick(value, axis, index):
    return lax.dynamic_index_in_dim(value, index, axis, keepdims=False)


def in_order(core, mine, other):
    first = core == 0
    return (jnp.where(first, mine, other), jnp.where(first, other, mine))


def core_sum(value):
    return value + swap(bfloat(value), 1, 0).astype(jnp.float32)


def core_columns(value, lead):
    seq_count = lax.axis_size("seq")
    total = value.shape[-1]
    chunk = total // seq_count
    parts = value.reshape(value.shape[:-1] + (seq_count // (2 * lead), 2, lead * chunk))
    flat = value.shape[:-1] + (total // 2,)
    return (parts[..., 0, :].reshape(flat), parts[..., 1, :].reshape(flat))


def plane_steps(stacks, orders, firsts):
    labels = [[0] for _ in stacks]
    for turn in range(len(orders[0])):
        got = [swap(stack, bits[turn], 0) for stack, bits in zip(stacks, orders)]
        done = yield list(stacks) + got
        stacks, got = done[: len(stacks)], done[len(stacks) :]
        fresh = [[label | bits[turn] for label in old] for old, bits in zip(labels, orders)]
        if turn == len(orders[0]) - 1:
            break
        stacks = [jnp.concatenate(pair) for pair in zip(stacks, got)]
        labels = [old + new for old, new in zip(labels, fresh)]
    return [
        piece
        for old, new, first, stack, other in zip(labels, fresh, firsts, stacks, got)
        for piece in ((old, first, stack), (new, first, other))
    ]


def column_first_steps(own):
    (column,) = yield [lax.all_gather(own, "kv")]
    half = column.shape[0] // 2
    x_bits, y_bits = plane_bits()
    orders = (x_bits + y_bits, y_bits + x_bits)
    return (yield from plane_steps([column[None, :half], column[None, half:]], orders, (0, half)))


def plane_first_steps(own):
    x_bits, y_bits = plane_bits()
    half = own.shape[1] // 2
    orders = (x_bits + y_bits, y_bits + x_bits)
    parts = [own[None, None, :, :half], own[None, None, :, half:]]
    pieces = yield from plane_steps(parts, orders, (0, 0))
    stacks = []
    for first, second in (pieces[:2], pieces[2:]):
        labels = first[0] + second[0]
        stack = jnp.concatenate([first[2], second[2]])[:, 0]
        stacks.append(jnp.stack([stack[labels.index(label)] for label in sorted(labels)]))
    return (sorted(labels), jnp.concatenate(stacks, 2))


def run_rounds(starts, extras):
    live = {}
    results = {}
    turn = 0
    made = {}
    while turn < len(starts) or live:
        if turn < len(starts):
            for name, steps in starts[turn](made):
                live[name] = (steps, None)
        values, spans = [], {}
        for name, (steps, sent) in list(live.items()):
            try:
                out = steps.send(sent)
            except StopIteration as stop:
                results[name] = stop.value
                made[name] = stop.value
                del live[name]
                continue
            spans[name] = (len(values), len(values) + len(out))
            values += out
        if not values:
            turn += 1
            continue
        more = extras.get(turn, lambda made: {})(made)
        names = list(more)
        leaves, shape = jax.tree.flatten([more[name] for name in names])
        values = lax.optimization_barrier(tuple(values) + tuple(leaves))
        for name, (first, last) in spans.items():
            live[name] = (live[name][0], list(values[first:last]))
        made.update(zip(names, jax.tree.unflatten(shape, values[len(values) - len(leaves) :])))
        made["tie"] = values[0]
        turn += 1
    return results, made


def place_kernel(plan, form, where_ref, *refs):
    sources = refs[: len(plan)]
    count = (len(refs) - len(plan) - 2) // 2
    targets = refs[len(plan) : len(plan) + count]
    staged = refs[len(plan) + count : len(plan) + 2 * count]
    in_sems, out_sems = refs[-2:]
    own = where_ref[0]
    kind = where_ref[1]
    copies = []
    for source, (labels, first) in zip(sources, plan):
        for place, label in enumerate(labels):
            chip = own ^ (label // 2)
            for step in range(source.shape[1]):
                block = source.at[place, step]
                z = first + step
                if form == "attention":
                    split = staged[0].shape[-1]
                    half = staged[1].shape[-1]
                    for side in range(2):
                        copies.append((block.at[side, :, :split], 0, (chip, side, z)))
                        copies.append((block.at[side, :, split:], 1, (side, chip, z)))
                elif form == "first":
                    for side in range(2):
                        copies.append((block.at[side], 0, (chip, side, z)))
                elif form == "second":
                    copies.append((block.at[0], 0, (chip, z)))
                else:
                    for layer in range(2):
                        down = block.at[2 * layer + kind]
                        for side in range(2):
                            copies.append((down.at[side], 0, (layer, chip, side, z)))
                        up = block.at[4 + 2 * layer + kind]
                        for fold in range(4):
                            copies.append((up.at[fold // 2, fold % 2], 1, (layer, fold, chip, z)))
    started = []
    for place, (origin, turn, index) in enumerate(copies):
        copy = pltpu.make_async_copy(origin, staged[turn].at[index], in_sems.at[place])
        copy.start()
        started.append(copy)
    ended = []
    for place, (origin, turn, index) in enumerate(copies):
        started[place].wait()
        copy = pltpu.make_async_copy(
            staged[turn].at[index], targets[turn].at[index], out_sems.at[place]
        )
        copy.start()
        ended.append(copy)
    for copy in ended:
        copy.wait()


def place_blocks(pieces, where, form, shapes):
    plan = [(labels, first) for labels, first, _ in pieces]
    blocks = sum(len(labels) * stack.shape[1] for labels, _, stack in pieces)
    copies = blocks * {"attention": 4, "first": 2, "second": 1, "adapter": 12}[form]
    anywhere = pl.BlockSpec(memory_space=pl.ANY)
    return pl.pallas_call(
        functools.partial(place_kernel, plan, form),
        grid_spec=pltpu.PrefetchScalarGridSpec(
            num_scalar_prefetch=1,
            grid=(1,),
            in_specs=[anywhere] * len(pieces),
            out_specs=[anywhere] * len(shapes),
            scratch_shapes=[pltpu.VMEM(shape, jnp.bfloat16) for shape in shapes]
            + [pltpu.SemaphoreType.DMA((copies,))] * 2,
        ),
        out_shape=[jax.ShapeDtypeStruct(shape, jnp.bfloat16) for shape in shapes],
        compiler_params=pltpu.CompilerParams(vmem_limit_bytes=24 * MEBI),
        cost_estimate=LIGHT,
    )(where, *[stack for _, _, stack in pieces])


def head_scores(length, causal, query, keys):
    scores = times_second(query, keys) * score_scale
    key = lax.broadcasted_iota(jnp.int32, scores.shape, 1)
    mask = key < length
    if causal:
        mask = mask & (key <= lax.broadcasted_iota(jnp.int32, scores.shape, 0))
    return jnp.where(mask, scores, -1000000000.0)


def softmax(scores):
    weights = jnp.exp(scores - jnp.max(scores, 1, keepdims=True))
    return weights * (1.0 / jnp.sum(weights, 1, keepdims=True))


def one_head(value, head):
    lane = lax.broadcasted_iota(jnp.int32, value.shape, 1)
    return jnp.where(lane // HDIM == head, value, jnp.zeros((), value.dtype))


def attention_kernel(causal, length_ref, query_ref, key_ref, value_ref, out_ref):
    query, keys, values = query_ref[...], key_ref[...], value_ref[...]
    out = jnp.zeros(out_ref.shape, jnp.float32)
    for head in range(query.shape[1] // HDIM):
        scores = head_scores(length_ref[0], causal, query, one_head(keys, head))
        out = out + times_plain(bfloat(softmax(scores)), one_head(values, head))
    out_ref[...] = bfloat(out)


def attention_grad_kernel(
    causal, length_ref, query_ref, key_ref, value_ref, out_ref, query_out, key_out, value_out
):
    query, keys, values, out_grad = query_ref[...], key_ref[...], value_ref[...], out_ref[...]
    query_grad = jnp.zeros(query.shape, jnp.float32)
    key_grad = jnp.zeros(keys.shape, jnp.float32)
    value_grad = jnp.zeros(values.shape, jnp.float32)
    for head in range(query.shape[1] // HDIM):
        head_keys = one_head(keys, head)
        head_out = one_head(out_grad, head)
        probs = softmax(head_scores(length_ref[0], causal, query, head_keys))
        prob_grad = times_second(head_out, values)
        spread = jnp.sum(probs * prob_grad, 1, keepdims=True)
        score_grad = bfloat(probs * (prob_grad - spread))
        value_grad = value_grad + times_first(bfloat(probs), head_out)
        query_grad = query_grad + times_plain(score_grad, head_keys)
        key_grad = key_grad + times_first(score_grad, one_head(query, head))
    query_out[...] = bfloat(query_grad * score_scale)
    key_out[...] = bfloat(key_grad * score_scale)
    value_out[...] = bfloat(value_grad)


def attention_call(kernel, length, causal, arrays, outs):
    lanes = 2 * HDIM
    columns = outs[0][1]

    def spec(rows, first):
        return pl.BlockSpec((rows, lanes), lambda i, _: (0, i + first // lanes))

    return pl.pallas_call(
        functools.partial(kernel, causal),
        grid_spec=pltpu.PrefetchScalarGridSpec(
            num_scalar_prefetch=1,
            grid=(columns // lanes,),
            in_specs=[spec(array.shape[0], first) for array, first in arrays],
            out_specs=[spec(rows, 0) for rows, _ in outs],
        ),
        out_shape=[jax.ShapeDtypeStruct(out, jnp.bfloat16) for out in outs],
        compiler_params=pltpu.CompilerParams(vmem_limit_bytes=48 * MEBI),
        cost_estimate=LIGHT,
    )(length.reshape(1), *[array for array, _ in arrays])


def attend(length, causal, query, pair):
    rows = query[0].shape[0]
    width = pair[0].shape[1] - pair[1]
    half = width // 2
    arrays = [query, pair, (pair[0], pair[1] + half)]
    return attention_call(attention_kernel, length, causal, arrays, [(rows, half)])[0]


def attend_back(length, causal, query, pair, out_grad):
    rows = query[0].shape[0]
    keys = pair[0].shape[0]
    half = (pair[0].shape[1] - pair[1]) // 2
    arrays = [query, pair, (pair[0], pair[1] + half), (out_grad, 0)]
    outs = [(rows, half), (keys, half), (keys, half)]
    return attention_call(attention_grad_kernel, length, causal, arrays, outs)


def gelu_pair(value):
    phi = 0.5 * (1.0 + lax.erf(value * 0.7071067811865476))
    slope = phi + value * jnp.exp(-0.5 * value * value) * 0.3989422804014327
    return lax.optimization_barrier((bfloat(value * phi), slope))


def feed_forward(low_in, w_first, w_second, down, upward):
    hidden = times_plain(low_in, w_first)
    inner = times_plain(low_in, down)
    hidden_low, slope = gelu_pair(hidden)
    inner_low, inner_slope = gelu_pair(inner)
    branch = times_plain(hidden_low, w_second) + 4.0 * times_plain(inner_low, upward)
    return (branch, (low_in, slope, inner_slope, inner_low))


def feed_backward(grad, cache, w_first, w_second, down, upward):
    low_in, slope, inner_slope, inner_low = cache
    hidden_grad = bfloat(times_second(bfloat(grad), w_second) * slope)
    adapter_grad = bfloat(4.0 * grad)
    upward_grad = times_first(inner_low, adapter_grad)
    inner_grad = bfloat(times_second(adapter_grad, upward) * inner_slope)
    down_grad = times_first(low_in, inner_grad)
    value_grad = times_second(hidden_grad, w_first) + times_second(inner_grad, down)
    return (value_grad, down_grad, upward_grad)


def vocab_kernel(
    count, tile, step, order_ref, rows_ref, table_ref, mixed_ref, stats_ref,
    scores, table, mixed, stats, table_sems, out_sems,
):
    parts = step // LIVE_ROWS
    turn = pl.program_id(0)
    alive = order_ref[order_ref.shape[0] - 1]
    padded = table.shape[0]
    tiles = range(0, padded, tile)

    def table_copy(place):
        span = slice(place * tile, (place + 1) * tile)
        return pltpu.make_async_copy(table_ref.at[span], table.at[span], table_sems.at[place])

    def out_copies(first):
        copies = []
        for part in range(parts):
            row = pl.multiple_of(order_ref[first + part] * LIVE_ROWS, LIVE_ROWS)
            span = slice(part * LIVE_ROWS, (part + 1) * LIVE_ROWS)
            for place, (origin, target) in enumerate(((mixed, mixed_ref), (stats, stats_ref))):
                copies.append(
                    pltpu.make_async_copy(
                        origin.at[span],
                        target.at[pl.ds(row, LIVE_ROWS)],
                        out_sems.at[place, part],
                    )
                )
        return copies

    @pl.when(turn == 0)
    def _():
        for place in range(len(tiles)):
            table_copy(place).start()
        for place in range(len(tiles)):
            table_copy(place).wait()

    first = turn * parts

    @pl.when(first < alive)
    def _():
        places = [
            pl.ds(pl.multiple_of(order_ref[first + part] * LIVE_ROWS, LIVE_ROWS), LIVE_ROWS)
            for part in range(parts)
        ]
        rows = jnp.concatenate([rows_ref[place, :] for place in places])
        top = jnp.full((step, 1), LOWEST, jnp.float32)
        for start in tiles:
            part = times_second(rows, table[start : start + tile, :])
            if start + tile > count:
                entry = lax.broadcasted_iota(jnp.int32, part.shape, 1) + start
                part = jnp.where(entry < count, part, LOWEST)
            scores[:, start : start + tile] = part
            top = jnp.maximum(top, jnp.max(part, 1, keepdims=True))
        total = jnp.zeros((step, 1), jnp.float32)
        mix = jnp.zeros((step, rows.shape[1]), jnp.float32)
        for start in tiles:
            weights = jnp.exp(scores[:, start : start + tile] - top)
            total = total + jnp.sum(weights, 1, keepdims=True)
            mix = mix + times_plain(bfloat(weights), table[start : start + tile, :])

        @pl.when(turn > 0)
        def _():
            for copy in out_copies(first - parts):
                copy.wait()

        mixed[...] = mix
        stats[...] = jnp.concatenate(
            [jnp.broadcast_to(top, (step, 64)), jnp.broadcast_to(total, (step, 64))], 1
        )
        for copy in out_copies(first):
            copy.start()

        @pl.when(first + parts >= alive)
        def _():
            for copy in out_copies(first):
                copy.wait()


def vocab_pass(rows, live_blocks, table, count, step, tile):
    total, width = rows.shape
    padded = table.shape[0]
    flags = live_blocks.astype(jnp.int32)
    alive_count = jnp.sum(flags)
    rank = jnp.where(
        live_blocks, jnp.cumsum(flags) - 1, alive_count + jnp.cumsum(1 - flags) - 1
    )
    ids = jnp.arange(flags.shape[0], dtype=jnp.int32)
    order = jnp.sum(jnp.where(rank[None, :] == ids[:, None], ids[None, :], 0), 1)
    order = jnp.concatenate([order, alive_count[None]]).astype(jnp.int32)

    anywhere = pl.BlockSpec(memory_space=pl.ANY)
    return pl.pallas_call(
        functools.partial(vocab_kernel, count, tile, step),
        grid_spec=pltpu.PrefetchScalarGridSpec(
            num_scalar_prefetch=1,
            grid=(total // step,),
            in_specs=[
                pl.BlockSpec((total, width), lambda i, _: (0, 0), pipeline_mode=pl.Buffered(1)),
                anywhere,
            ],
            out_specs=[anywhere, anywhere],
            scratch_shapes=[
                pltpu.VMEM((step, padded), jnp.float32),
                pltpu.VMEM((padded, width), jnp.bfloat16),
                pltpu.VMEM((step, width), jnp.float32),
                pltpu.VMEM((step, 128), jnp.float32),
                pltpu.SemaphoreType.DMA((padded // tile,)),
                pltpu.SemaphoreType.DMA((2, step // LIVE_ROWS)),
            ],
        ),
        out_shape=[
            jax.ShapeDtypeStruct((total, width), jnp.float32),
            jax.ShapeDtypeStruct((total, 128), jnp.float32),
        ],
        compiler_params=pltpu.CompilerParams(vmem_limit_bytes=56 * MEBI),
        cost_estimate=pl.CostEstimate(
            flops=3 * total * width * padded,
            bytes_accessed=2 * padded * width + 6 * total * width,
            transcendentals=total * padded,
        ),
    )(order, rows, table)


def exchange(values, bits):
    got = [swap(value, bit, 0) for value, bit in zip(values, bits)]
    return lax.optimization_barrier(got)


def spread(halves, orders):
    halves = [{0: half} for half in halves]
    for turn in range(len(orders[0])):
        keys = sorted(halves[0])
        got = exchange(
            [jnp.stack([half[k] for k in sorted(half)]) for half in halves],
            [bits[turn] for bits in orders],
        )
        halves = [
            half | {key | bits[turn]: other[place] for place, key in enumerate(sorted(half))}
            for half, other, bits in zip(halves, got, orders)
        ]
    return halves


def halved_sum(halves, orders):
    for turn in range(len(orders[0])):
        sent, kept = [], []
        for half, bits in zip(halves, orders):
            keep = [key for key in sorted(half) if not key & bits[turn]]
            kept.append(keep)
            sent.append(jnp.stack([bfloat(half[key | bits[turn]]) for key in keep]))
        got = exchange(sent, [bits[turn] for bits in orders])
        halves = [
            {key: half[key] + other[place].astype(jnp.float32) for place, key in enumerate(keep)}
            for half, keep, other in zip(halves, kept, got)
        ]
    return [half[0] for half in halves]


def merged_sum(halves, orders):
    for turn in range(len(orders[0])):
        sent, kept = [], []
        for half, bits in zip(halves, orders):
            keep = [key for key in sorted(half) if not key & bits[turn]]
            kept.append(keep)
            away = [half[key | bits[turn]] for key in keep]
            sent.append(jnp.stack([bfloat(mix) for mix, _ in away]))
            sent.append(jnp.stack([stats for _, stats in away]))
        got = exchange(sent, [bits[turn] for bits in orders for _ in range(2)])
        merged = []
        for place, (half, keep) in enumerate(zip(halves, kept)):
            mixes, stats = got[2 * place], got[2 * place + 1]
            blocks = {}
            for index, key in enumerate(keep):
                mix, (top, total) = half[key]
                other_top, other_total = stats[index]
                best = jnp.maximum(top, other_top)
                scale = jnp.exp(top - best)
                other_scale = jnp.exp(other_top - best)
                mix = mix * scale[:, None] + mixes[index].astype(jnp.float32) * other_scale[:, None]
                total = total * scale + other_total * other_scale
                blocks[key] = (mix, jnp.stack([best, total]))
            merged.append(blocks)
        halves = merged
    return [half[0] for half in halves]


def adapter_steps(down_grad, up_grad, kind, tasks, lead):
    seq_count, kv_count = lax.axis_size("seq"), lax.axis_size("kv")
    seq_index, kv_index = lax.axis_index("seq"), lax.axis_index("kv")
    chips = seq_count // 2
    devices = seq_count * kv_count
    core = seq_index % 2
    lanes = down_grad.shape[1]
    down_rows = down_grad.shape[0] // devices
    up_rows = up_grad.shape[0] // (chips * kv_count)
    folds = up_grad.shape[1] // lanes
    down_part = down_grad.reshape(chips, 2, kv_count, down_rows, lanes)
    up_part = up_grad.reshape(chips, kv_count, up_rows, folds, lanes).transpose(0, 1, 3, 2, 4)
    up_part = up_part.reshape(chips, kv_count, folds * up_rows, lanes)
    mine, other, up_part = yield [
        pick(down_part, 1, core),
        swap(bfloat(pick(down_part, 1, 1 - core)), 1, 0),
        up_part,
    ]
    grad = jnp.concatenate([mine, other.astype(jnp.float32), up_part], 2)
    height = grad.shape[2]
    x_bits, y_bits = plane_bits()
    orders = [(x_bits + y_bits, y_bits + x_bits)[task % 2] for task in range(tasks)]
    lefts = [list(reversed(x_bits + y_bits)) for _ in range(tasks)]
    parts = []
    for task in range(tasks):
        part = grad * (kind == task).astype(jnp.float32)
        parts.append(
            part.reshape([2] * (len(x_bits) + len(y_bits)) + [kv_count, height, lanes])
        )
    for turn in range(len(orders[0])):
        kept, got = [], []
        for part, bits, left in zip(parts, orders, lefts):
            bit = bits[turn]
            axis = left.index(bit)
            left.remove(bit)
            place = (seq_index // bit) % 2
            kept.append(pick(part, axis, place))
            got.append(swap(bfloat(pick(part, axis, 1 - place)), bit, 0))
        done = yield kept + got
        parts = [
            part + other.astype(jnp.float32) for part, other in zip(done[:tasks], done[tasks:])
        ]
    part = jnp.stack(parts, 1)
    done = yield [pick(part, 0, kv_index)] + [
        swap(bfloat(pick(part, 0, kv_index ^ step)), 0, step) for step in range(1, kv_count)
    ]
    total = done[0]
    for other in done[1:]:
        total = total + other.astype(jnp.float32)
    sides = in_order(core, total[:, :down_rows], total[:, down_rows : 2 * down_rows])
    sides = [
        side.reshape(tasks, down_rows, seq_count // (2 * lead), lanes * 2 * lead // seq_count)
        for side in sides
    ]
    down_total = jnp.stack(sides, 3).reshape(tasks, down_rows, 2 * lanes)
    up_total = total[:, 2 * down_rows :].reshape(tasks, folds, up_rows, lanes)
    up_total = up_total.transpose(0, 2, 1, 3).reshape(tasks, up_rows, folds * lanes)
    if lead == 2:
        up_total = trade_bits(up_total)
    return (down_total, up_total)


class Steps:
    def __init__(self, steps):
        self.steps = steps
        self.sent = next(steps)
        self.result = None

    def after(self, value):
        if self.result is not None:
            return
        count = len(self.sent)
        try:
            self.sent = self.steps.send(
                list(lax.optimization_barrier(tuple(self.sent) + (value,))[:count])
            )
        except StopIteration as stop:
            self.result = stop.value

    def finish(self):
        while self.result is None:
            try:
                self.sent = self.steps.send(self.sent)
            except StopIteration as stop:
                self.result = stop.value
        return self.result


def total_sum(value):
    step = 1
    while step < lax.axis_size("seq"):
        value = value + swap(value, step, 0)
        step *= 2
    step = 1
    while step < lax.axis_size("kv"):
        value = value + swap(value, 0, step)
        step *= 2
    return value


def item_rows(embeds):
    seq_count, kv_count = lax.axis_size("seq"), lax.axis_size("kv")
    seq_index, kv_index = lax.axis_index("seq"), lax.axis_index("kv")
    got = []
    for turn in range(2):
        pairs = []
        for s in range(seq_count):
            for z in range(kv_count):
                source = (s - s % 2 + z % 2) * kv_count + 2 * (s % 2) + ((z // 2) ^ turn)
                pairs.append((source, s * kv_count + z))
        sent = pick(embeds[:, 0], 0, (kv_index % 2) ^ turn)
        got.append(lax.ppermute(sent, AXES, pairs))
    swapped = kv_index // 2 == 1
    mine = jnp.concatenate(
        [jnp.where(swapped, got[1], got[0]), jnp.where(swapped, got[0], got[1])]
    )
    return jnp.concatenate(in_order(seq_index % 2, mine, swap(mine, 1, 0)))


def adam_update(weight, first, second, grad, rate, decay, count_step):
    first_new = beta_one * first + (1.0 - beta_one) * grad
    second_new = beta_two * second + (1.0 - beta_two) * grad * grad
    first_hat = first_new / (1.0 - jnp.power(beta_one, count_step))
    second_hat = second_new / (1.0 - jnp.power(beta_two, count_step))
    weight_new = weight - rate * (
        first_hat / (jnp.sqrt(second_hat) + adam_epsilon) + decay * weight
    )
    return (weight_new, first_new, second_new)


def per_device(
    src_embed,
    tgt_embed,
    targets,
    src_len,
    tgt_len,
    task,
    step,
    attn_in,
    attn_out,
    ffn_in,
    ffn_out,
    embed,
    down_w,
    down_m,
    down_v,
    up_w,
    up_m,
    up_v,
    norm_params,
    norm_m,
    norm_v,
):
    seq_count, kv_count = lax.axis_size("seq"), lax.axis_size("kv")
    seq_index, kv_index = lax.axis_index("seq"), lax.axis_index("kv")
    chips = seq_count // 2
    devices = seq_count * kv_count
    width = attn_out.shape[2]
    hidden = ffn_in.shape[2]
    bottleneck = down_w.shape[3]
    tasks = down_w.shape[1]
    vocab_rows = embed.shape[0]
    vocab_total = vocab_rows * seq_count
    core = seq_index % 2
    batch = kv_index // 2
    item = seq_index - core + kv_index % 2
    source_length = src_len[batch, item]
    target_length = tgt_len[batch, item]
    kind = task[batch, item]
    count = jnp.sum(tgt_len).astype(jnp.float32)
    gains = norm_params[0]
    biases = norm_params[1]

    x_bits, y_bits = plane_bits()
    orders = (x_bits + y_bits, y_bits + x_bits)
    share = width // devices
    lead = 1 if kv_count * share % HDIM == 0 else 2
    sides = [
        core_columns(part, lead)
        for part in (
            [attn_in[j].reshape(share, 3, width) for j in range(3)]
            + [ffn_in[0], ffn_in[1]]
            + [bfloat(down_w[l, t]) for l in range(2) for t in range(tasks)]
        )
    ]
    flat = [jnp.concatenate([part[c].reshape(share, -1) for part in sides], 1) for c in range(2)]
    mine = jnp.where(core == 0, flat[0], flat[1])
    theirs = swap(jnp.where(core == 0, flat[1], flat[0]), 1, 0)
    split = jnp.stack(in_order(core, mine, theirs))
    edges = [0]
    for part in sides:
        edges.append(edges[-1] + part[0].size // share)
    split = [split[:, :, first:last] for first, last in zip(edges, edges[1:])]
    out_low, second_low, up_low = attn_out, ffn_out, bfloat(up_w)
    if lead == 2:
        out_low, second_low, up_low = trade_bits((out_low, second_low, up_low))
    half_w = width // 2
    own_attn = [
        jnp.concatenate(
            [split[j], out_low[j].reshape(share, 2, half_w).transpose(1, 0, 2)], 2
        )
        for j in range(3)
    ]
    lanes = bottleneck // 2
    up_rows = up_w.shape[2]
    own_down = jnp.stack(split[5:]).reshape(2 * tasks, 2, 2, share // 2, lanes)
    own_up = up_low.reshape(2 * tasks, up_rows, 4, lanes).transpose(0, 2, 1, 3)
    own_adapter = jnp.concatenate([own_down, own_up.reshape(2 * tasks, 2, 2, up_rows, lanes)])
    attn_shapes = [
        (chips, 2, kv_count, share, 3 * half_w),
        (2, chips, kv_count, share, half_w),
    ]
    first_shapes = [(chips, 2, kv_count, share, hidden // 2)]
    second_shapes = [(chips, kv_count, hidden // devices, width)]
    adapter_shapes = [
        (2, chips, 2, kv_count, 2, share // 2, lanes),
        (2, 4, chips, kv_count, up_rows, lanes),
    ]
    groups = [
        (second_low[0][None], "second", second_shapes),
        (own_attn[0], "attention", attn_shapes),
        (own_attn[1], "attention", attn_shapes),
        (split[3], "first", first_shapes),
        (own_adapter, "adapter", adapter_shapes),
        (own_attn[2], "attention", attn_shapes),
        (split[4], "first", first_shapes),
        (second_low[1][None], "second", second_shapes),
    ]
    where = jnp.stack([seq_index // 2, kind]).astype(jnp.int32)
    tile = 1280

    def column_start(place):
        return lambda made: [(place, column_first_steps(groups[place][0]))]

    def with_last(made):
        return [
            (len(groups) - 1, plane_first_steps(groups[-1][0])),
            (0, column_first_steps(groups[0][0])),
        ]

    def ids_in(made):
        parts = [pick(targets, 0, batch)]
        for turn in range(1, kv_count):
            parts.append(swap(pick(targets, 0, batch ^ (turn // 2)), 0, turn))
        order = kv_index ^ jnp.arange(kv_count, dtype=jnp.int32)
        chosen = order[:, None] == jnp.arange(kv_count, dtype=jnp.int32)[None, :]
        parts = jnp.sum(jnp.where(chosen[:, :, None, None], jnp.stack(parts)[:, None], 0), 0)
        return {"ids": parts.transpose(1, 0, 2)}

    def rows_in(made):
        return {
            "source": item_rows(src_embed),
            "target": item_rows(tgt_embed),
        }

    def table_in(made):
        low = after(embed, made["tie"])
        return {"table": jnp.pad(low, ((0, -vocab_rows % tile), (0, 0)))}

    def sum_in(made):
        return {"table_sum": jnp.sum(after(embed, made["tie"]).astype(jnp.float32), 0)}

    own_rows = tgt_embed.shape[2] * kv_count // 2
    half = own_rows // 2
    relative = seq_index ^ jnp.arange(seq_count, dtype=jnp.int32)
    row_items = relative - relative % 2 + kv_index % 2
    row_pos = (
        (relative % 2)[None, :, None] * own_rows
        + jnp.arange(2, dtype=jnp.int32)[:, None, None] * half
        + jnp.arange(half, dtype=jnp.int32)[None, None, :]
    )
    plane_lengths = pick(tgt_len, 0, batch)
    plane_lengths = jnp.sum(
        jnp.where(row_items[:, None] == jnp.arange(seq_count)[None, :], plane_lengths[None], 0), 1
    )
    alive = row_pos < plane_lengths[None, :, None]
    live = alive.astype(jnp.float32) / count

    def linear_in(made):
        ids = made["ids"].reshape(seq_count, 2, 2, half)
        chosen = (row_items[:, None] == jnp.arange(seq_count)[None, :])[:, :, None] & (
            (relative % 2)[:, None, None] == jnp.arange(2)[None, None, :]
        )
        row_ids = jnp.sum(jnp.where(chosen[:, :, :, None, None], ids[None], 0), (1, 2))
        row_ids = row_ids.transpose(1, 0, 2).reshape(-1)
        local_ids = after(row_ids - seq_index * vocab_rows, made["tie"])
        local_hit = (local_ids >= 0) & (local_ids < vocab_rows)
        target_rows = jnp.take(embed, jnp.clip(local_ids, 0, vocab_rows - 1), axis=0)
        linear = bfloat(
            jnp.where(local_hit[:, None], 0.9 * target_rows.astype(jnp.float32), 0.0)
            + (0.1 / vocab_total) * made["table_sum"][None]
        )
        return {"linear": linear.reshape(2, seq_count, half, width)}

    def last_in(made):
        return {"last": step + 0}

    starts = [with_last] + [column_start(place) for place in range(1, len(groups) - 1)]
    def place(made, group):
        _, form, shape = groups[group]
        return place_blocks(made[group], where, form, shape)

    def attention_weights(made, group):
        w_in, w_out = place(made, group)
        w_out = jnp.concatenate(list(w_out.reshape(2, half_w, half_w)), 1)
        return (w_in.reshape(width, 3 * half_w), w_out)

    def encoder_attention(made):
        w_in, w_out = attention_weights(made, 1)
        x0, cache = norm_forward(made["source"].astype(jnp.float32), gains[0], biases[0])
        pair = bfloat(times_plain(bfloat(x0), w_in))
        out = attend(source_length, False, (pair, 0), (pair, half_w))
        return {
            "enc": (x0, cache, pair, times_plain(out, w_out)),
            "enc_w": (w_in, w_out),
        }

    def decoder_attention(made):
        x0, cache0, pair, part = made["enc"]
        x1, cache1 = norm_forward(x0 + core_sum(part), gains[1], biases[1])
        w_in, w_out = attention_weights(made, 2)
        y0, cache3 = norm_forward(made["target"].astype(jnp.float32), gains[3], biases[3])
        self_pair = bfloat(times_plain(bfloat(y0), w_in))
        out = attend(target_length, True, (self_pair, 0), (self_pair, half_w))
        return {
            "x1": (x1, cache1),
            "dec": (y0, cache3, self_pair, times_plain(out, w_out)),
            "dec_w": (w_in, w_out),
        }

    def encoder_hidden(made):
        y0, cache3, self_pair, part = made["dec"]
        y1, cache4 = norm_forward(y0 + core_sum(part), gains[4], biases[4])
        first = place(made, 3)[0].reshape(width, hidden // 2)
        low_in = bfloat(made["x1"][0])
        return {
            "y1": (y1, cache4),
            "first0": first,
            "hidden0": (low_in,) + gelu_pair(times_plain(low_in, first)),
        }

    def encoder_branch(made):
        down_all, up_all = place(made, 4)
        down_all = down_all.reshape(2, width, lanes)
        up_all = up_all.reshape(2, 4, lanes, lanes)
        up_all = jnp.concatenate([up_all[:, fold] for fold in range(4)], 2)
        second = place(made, 0)[0].reshape(hidden // 2, width)
        low_in, hidden_low, slope = made["hidden0"]
        inner_low, inner_slope = gelu_pair(times_plain(low_in, down_all[0]))
        part = times_plain(hidden_low, second) + 4.0 * times_plain(inner_low, up_all[0])
        return {
            "adapters": (down_all, up_all),
            "second0": second,
            "feed0": (part, (low_in, slope, inner_slope, inner_low)),
        }

    def cross_attention(made):
        x2, cache2 = norm_forward(made["x1"][0] + core_sum(made["feed0"][0]), gains[2], biases[2])
        w_in, w_out = attention_weights(made, 5)
        cross_query = bfloat(times_plain(bfloat(made["y1"][0]), w_in[:, :half_w]))
        cross_pair = bfloat(times_plain(bfloat(x2), w_in[:, half_w:]))
        out = attend(source_length, False, (cross_query, 0), (cross_pair, 0))
        return {
            "cross": (cache2, cross_query, cross_pair, times_plain(out, w_out)),
            "cross_w": (w_in, w_out),
        }

    extras = {
        0: rows_in,
        1: ids_in,
        2: table_in,
        3: sum_in,
        4: encoder_attention,
        5: decoder_attention,
        6: lambda made: encoder_hidden(made) | last_in(made),
        7: encoder_branch,
        8: cross_attention,
    }
    late = len(x_bits + y_bits) - 2
    extras = {turn + (late if turn > 3 else 0): value for turn, value in extras.items()}
    if late:
        extras[4] = linear_in
    else:
        attention_first = extras[4]
        extras[4] = lambda made: attention_first(made) | linear_in(made)
    gathered, made = run_rounds(starts, extras)
    table, linear = made["table"], made["linear"]
    x0, cache0, enc_pair, _ = made["enc"]
    x1, cache1 = made["x1"]
    y0, cache3, self_pair, _ = made["dec"]
    y1, cache4 = made["y1"]
    cache2, cross_query, cross_pair, part = made["cross"]
    down_all, up_all = made["adapters"]
    enc_feed = made["feed0"][1]
    attn_w = [made["enc_w"], made["dec_w"], made["cross_w"]]
    y2, cache5 = norm_forward(y1 + core_sum(part), gains[5], biases[5])
    first_w = [made["first0"], place(gathered, 6)[0].reshape(width, hidden // 2)]
    labels, stack = gathered[len(groups) - 1]
    stack = lax.all_gather(after(stack, made["last"]), "kv", axis=1)
    second_w = place({7: [(labels, 0, stack)]}, 7)[0].reshape(hidden // 2, width)
    second_w = [made["second0"], second_w]
    branch, dec_feed = feed_forward(bfloat(y2), first_w[1], second_w[1], down_all[1], up_all[1])
    y3, cache6 = norm_forward(y2 + core_sum(branch), gains[6], biases[6])

    down_orders = [[1] + list(bits) for bits in orders]
    linear_sum = halved_sum(
        [
            {key: after(linear[h, key], made["tie"]) for key in range(seq_count)}
            for h in range(2)
        ],
        down_orders,
    )
    y3_low = bfloat(y3)
    near = [
        lax.dynamic_slice_in_dim(y3_low, place * own_rows + h * half, half)
        for h in range(2)
        for place in (core, 1 - core)
    ]
    far = spread([near[0], near[2]], [list(bits) + [1] for bits in orders])
    near = jnp.concatenate(near)
    far = jnp.concatenate([half_far[key] for half_far in far for key in range(2, seq_count)])
    blocks = [{}, {}]
    loss_part = 0.0
    for rows, first, last in ((near, 0, 2), (far, 2, seq_count)):
        flags = jnp.any(alive[:, first:last].reshape(-1, LIVE_ROWS), 1)
        mixed, stats = vocab_pass(rows, flags, table, vocab_rows, 256, tile)
        mixed = mixed.reshape(2, last - first, half, width)
        tops = stats[:, 0].reshape(2, last - first, half)
        totals = stats[:, 64].reshape(2, last - first, half)
        for h in range(2):
            for key in range(first, last):
                pair = jnp.stack([tops[h, key - first], totals[h, key - first]])
                blocks[h][key] = (mixed[h, key - first], pair)
        rows_alive = alive[:, first:last].astype(jnp.float32)[..., None]
        rows = rows.astype(jnp.float32).reshape(mixed.shape)
        loss_part = loss_part - jnp.sum(rows_alive * rows * linear[:, first:last].astype(jnp.float32))
    merged = merged_sum(blocks, down_orders)
    final_grad = []
    for h, (mix, (top, total)) in enumerate(merged):
        row_grad = (mix / total[:, None] - linear_sum[h]) * live[h, 0][:, None]
        final_grad.append(jnp.where(alive[h, 0][:, None], row_grad, 0.0))
        loss_part = loss_part + jnp.sum(jnp.where(alive[h, 0], top + jnp.log(total), 0.0))
    final_grad = bfloat(jnp.concatenate(final_grad))
    final_grad = jnp.concatenate(in_order(core, final_grad, swap(final_grad, 1, 0)))
    final_grad = final_grad.astype(jnp.float32)

    grad, grad6 = norm_backward(final_grad, cache6, gains[6])
    inner_grad, down_grad, up_grad = feed_backward(
        grad, dec_feed, first_w[1], second_w[1], down_all[1], up_all[1]
    )
    dec_steps = Steps(adapter_steps(down_grad, up_grad, kind, tasks, lead))
    grad, grad5 = norm_backward(grad + core_sum(inner_grad), cache5, gains[5])
    out_grad = bfloat(times_second(bfloat(grad), attn_w[2][1]))
    dec_steps.after(out_grad)
    dq, dk, dv = attend_back(source_length, False, (cross_query, 0), (cross_pair, 0), out_grad)
    enc_grad = times_second(jnp.concatenate([dk, dv], 1), attn_w[2][0][:, half_w:])
    query_grad = times_second(dq, attn_w[2][0][:, :half_w])
    dec_steps.after(dq)
    summed = core_sum(jnp.concatenate([enc_grad, query_grad]))
    enc_rows = x0.shape[0]
    dec_grad, grad4 = norm_backward(grad + summed[enc_rows:], cache4, gains[4])
    grad, grad2 = norm_backward(summed[:enc_rows], cache2, gains[2])
    inner_grad, down_grad, up_grad = feed_backward(
        grad, enc_feed, first_w[0], second_w[0], down_all[0], up_all[0]
    )
    dec_steps.after(inner_grad)
    enc_steps = Steps(adapter_steps(down_grad, up_grad, kind, tasks, lead))
    out_grad = bfloat(times_second(bfloat(dec_grad), attn_w[1][1]))
    parts = attend_back(target_length, True, (self_pair, 0), (self_pair, half_w), out_grad)
    enc_steps.after(out_grad)
    dec_steps.after(parts[0])
    self_grad = times_second(jnp.concatenate(parts, 1), attn_w[1][0])
    enc_steps.after(parts[0])
    _, grad3 = norm_backward(dec_grad + core_sum(self_grad), cache3, gains[3])
    grad, grad1 = norm_backward(grad + core_sum(inner_grad), cache1, gains[1])
    out_grad = bfloat(times_second(bfloat(grad), attn_w[0][1]))
    parts = attend_back(source_length, False, (enc_pair, 0), (enc_pair, half_w), out_grad)
    enc_steps.after(parts[0])
    enc_grad = times_second(jnp.concatenate(parts, 1), attn_w[0][0])
    _, grad0 = norm_backward(grad + core_sum(enc_grad), cache0, gains[0])
    enc_sums, dec_sums = enc_steps.finish(), dec_steps.finish()

    norm_grad = 0.5 * jnp.stack([grad0, grad1, grad2, grad3, grad4, grad5, grad6], 1)
    down_part = jnp.stack([enc_sums[0], dec_sums[0]])
    up_part = jnp.stack([enc_sums[1], dec_sums[1]])
    square = jnp.sum(down_part * down_part) + jnp.sum(up_part * up_part)
    scalars = jnp.zeros((1, width), jnp.float32).at[0, 0].set(loss_part).at[0, 1].set(square)
    summed = total_sum(jnp.concatenate([norm_grad.reshape(-1, width), scalars]))
    norm_sum = summed[:-1].reshape(norm_grad.shape)
    loss_sum = summed[-1, 0]
    grad_norm = jnp.sqrt(summed[-1, 1] + jnp.sum(norm_sum * norm_sum))
    factor = clip_limit / jnp.maximum(grad_norm, clip_limit)
    count_step = step[0].astype(jnp.float32)
    down_new = adam_update(
        down_w, down_m, down_v, factor * down_part, rate_adapter, weight_decay, count_step
    )
    up_new = adam_update(up_w, up_m, up_v, factor * up_part, rate_adapter, weight_decay, count_step)
    norm_grad_out = factor * norm_sum
    norm_new = adam_update(norm_params, norm_m, norm_v, norm_grad_out, rate_norm, 0.0, count_step)
    return (
        loss_sum,
        count,
        grad_norm,
        down_new[0],
        down_new[1],
        down_new[2],
        up_new[0],
        up_new[1],
        up_new[2],
        norm_new[0],
        norm_new[1],
        norm_new[2],
        norm_grad_out,
    )


def solution(mesh):
    placed = (
        P(None, "seq", "kv", None),
        P(None, "seq", "kv", None),
        P(None, None, "kv"),
        P(),
        P(),
        P(),
        P(),
        P(None, ("seq", "kv"), None),
        P(None, ("seq", "kv"), None),
        P(None, ("seq", "kv"), None),
        P(None, ("seq", "kv"), None),
        P("seq", None),
        P(None, None, ("seq", "kv"), None),
        P(None, None, ("seq", "kv"), None),
        P(None, None, ("seq", "kv"), None),
        P(None, None, ("seq", "kv"), None),
        P(None, None, ("seq", "kv"), None),
        P(None, None, ("seq", "kv"), None),
        P(),
        P(),
        P(),
    )
    return jax.shard_map(
        per_device,
        mesh=mesh,
        in_specs=placed,
        out_specs=(
            P(),
            P(),
            P(),
            P(None, None, ("seq", "kv"), None),
            P(None, None, ("seq", "kv"), None),
            P(None, None, ("seq", "kv"), None),
            P(None, None, ("seq", "kv"), None),
            P(None, None, ("seq", "kv"), None),
            P(None, None, ("seq", "kv"), None),
            P(),
            P(),
            P(),
            P(),
        ),
        check_vma=False,
    )
```

```python
import functools

import jax
import jax.numpy as jnp
from jax import lax
from jax.experimental import pallas as pl
from jax.experimental.pallas import tpu as pltpu
from jax.sharding import PartitionSpec as P

HDIM = 64


norm_epsilon = 1e-05
score_scale = 0.125
clip_limit = 0.02
beta_one = 0.9
beta_two = 0.999
adam_epsilon = 1e-08
rate_adapter = 0.03
rate_norm = 0.25
weight_decay = 0.01


def bfloat(value):
    return value.astype(jnp.bfloat16)


def times_plain(left, right):
    return jnp.dot(left, right, preferred_element_type=jnp.float32)


def times_first(left, right):
    return lax.dot_general(
        left, right, (((0,), (0,)), ((), ())), preferred_element_type=jnp.float32
    )


def times_second(left, right):
    return lax.dot_general(
        left, right, (((1,), (1,)), ((), ())), preferred_element_type=jnp.float32
    )


def norm_forward(value, gain, bias):
    centered = value - jnp.mean(value, -1, keepdims=True)
    inverse = lax.rsqrt(jnp.mean(centered * centered, -1, keepdims=True) + norm_epsilon)
    normed = centered * inverse
    return (normed * gain + bias, (normed, inverse))


def norm_backward(grad, cache, gain):
    normed, inverse = cache
    scaled = grad * gain
    value_grad = inverse * (
        scaled
        - jnp.mean(scaled, -1, keepdims=True)
        - normed * jnp.mean(scaled * normed, -1, keepdims=True)
    )
    return (value_grad, jnp.stack([jnp.sum(grad * normed, 0), jnp.sum(grad, 0)]))


def gelu_slope(value):
    return (
        0.5 * (1.0 + lax.erf(value * 0.7071067811865476))
        + value * jnp.exp(-0.5 * value * value) * 0.3989422804014327
    )


AXES = ("seq", "kv")
MEBI = 2**20
LOWEST = -3e38
LIVE_ROWS = 64
LIGHT = pl.CostEstimate(flops=1, bytes_accessed=1, transcendentals=0)


def swap(value, seq_mask, kv_mask):
    seq_count, kv_count = lax.axis_size("seq"), lax.axis_size("kv")
    pairs = [
        (s * kv_count + z, (s ^ seq_mask) * kv_count + (z ^ kv_mask))
        for s in range(seq_count)
        for z in range(kv_count)
    ]
    return lax.ppermute(value, AXES, pairs)


def trade_bits(value):
    seq_count, kv_count = lax.axis_size("seq"), lax.axis_size("kv")
    pairs = [
        (s * kv_count + z, (s - s % 4 + 2 * (s % 2) + s // 2 % 2) * kv_count + z)
        for s in range(seq_count)
        for z in range(kv_count)
    ]
    return lax.ppermute(value, AXES, pairs)


def plane_bits():
    count = lax.axis_size("seq").bit_length() - 2
    bits = [2 << place for place in range(count)]
    return (bits[: count // 2], bits[count // 2 :])


def after(value, earlier):
    return lax.optimization_barrier((value, earlier))[0]


def pick(value, axis, index):
    return lax.dynamic_index_in_dim(value, index, axis, keepdims=False)


def in_order(core, mine, other):
    first = core == 0
    return (jnp.where(first, mine, other), jnp.where(first, other, mine))


def core_sum(value):
    return value + swap(bfloat(value), 1, 0).astype(jnp.float32)


def core_columns(value, lead):
    seq_count = lax.axis_size("seq")
    total = value.shape[-1]
    chunk = total // seq_count
    parts = value.reshape(value.shape[:-1] + (seq_count // (2 * lead), 2, lead * chunk))
    flat = value.shape[:-1] + (total // 2,)
    return (parts[..., 0, :].reshape(flat), parts[..., 1, :].reshape(flat))


def plane_steps(stacks, orders, firsts):
    labels = [[0] for _ in stacks]
    for turn in range(len(orders[0])):
        got = [swap(stack, bits[turn], 0) for stack, bits in zip(stacks, orders)]
        done = yield list(stacks) + got
        stacks, got = done[: len(stacks)], done[len(stacks) :]
        fresh = [[label | bits[turn] for label in old] for old, bits in zip(labels, orders)]
        if turn == len(orders[0]) - 1:
            break
        stacks = [jnp.concatenate(pair) for pair in zip(stacks, got)]
        labels = [old + new for old, new in zip(labels, fresh)]
    return [
        piece
        for old, new, first, stack, other in zip(labels, fresh, firsts, stacks, got)
        for piece in ((old, first, stack), (new, first, other))
    ]


def column_first_steps(own):
    (column,) = yield [lax.all_gather(own, "kv")]
    half = column.shape[0] // 2
    x_bits, y_bits = plane_bits()
    orders = (x_bits + y_bits, y_bits + x_bits)
    return (yield from plane_steps([column[None, :half], column[None, half:]], orders, (0, half)))


def plane_first_steps(own):
    x_bits, y_bits = plane_bits()
    half = own.shape[1] // 2
    orders = (x_bits + y_bits, y_bits + x_bits)
    parts = [own[None, None, :, :half], own[None, None, :, half:]]
    pieces = yield from plane_steps(parts, orders, (0, 0))
    stacks = []
    for first, second in (pieces[:2], pieces[2:]):
        labels = first[0] + second[0]
        stack = jnp.concatenate([first[2], second[2]])[:, 0]
        stacks.append(jnp.stack([stack[labels.index(label)] for label in sorted(labels)]))
    return (sorted(labels), jnp.concatenate(stacks, 2))


def run_rounds(starts, extras):
    live = {}
    results = {}
    turn = 0
    made = {}
    while turn < len(starts) or live:
        if turn < len(starts):
            for name, steps in starts[turn](made):
                live[name] = (steps, None)
        values, spans = [], {}
        for name, (steps, sent) in list(live.items()):
            try:
                out = steps.send(sent)
            except StopIteration as stop:
                results[name] = stop.value
                made[name] = stop.value
                del live[name]
                continue
            spans[name] = (len(values), len(values) + len(out))
            values += out
        if not values:
            turn += 1
            continue
        more = extras.get(turn, lambda made: {})(made)
        names = list(more)
        leaves, shape = jax.tree.flatten([more[name] for name in names])
        values = lax.optimization_barrier(tuple(values) + tuple(leaves))
        for name, (first, last) in spans.items():
            live[name] = (live[name][0], list(values[first:last]))
        made.update(zip(names, jax.tree.unflatten(shape, values[len(values) - len(leaves) :])))
        made["tie"] = values[0]
        turn += 1
    return results, made


def place_kernel(plan, form, where_ref, *refs):
    sources = refs[: len(plan)]
    count = (len(refs) - len(plan) - 2) // 2
    targets = refs[len(plan) : len(plan) + count]
    staged = refs[len(plan) + count : len(plan) + 2 * count]
    in_sems, out_sems = refs[-2:]
    own = where_ref[0]
    kind = where_ref[1]
    copies = []
    for source, (labels, first) in zip(sources, plan):
        for place, label in enumerate(labels):
            chip = own ^ (label // 2)
            block = source.at[place]
            span = slice(first, first + source.shape[1])
            if form == "attention":
                split = staged[0].shape[-1]
                for side in range(2):
                    copies.append((block.at[:, side, :, :split], 0, (chip, side, span)))
                    copies.append((block.at[:, side, :, split:], 1, (side, chip, span)))
            elif form == "first":
                for side in range(2):
                    copies.append((block.at[:, side], 0, (chip, side, span)))
            elif form == "second":
                copies.append((block.at[:, 0], 0, (chip, span)))
            else:
                for layer in range(2):
                    for side in range(2):
                        down = block.at[:, 2 * layer + kind, side]
                        copies.append((down, 0, (layer, chip, side, span)))
                    for fold in range(4):
                        up = block.at[:, 4 + 2 * layer + kind, fold // 2, fold % 2]
                        copies.append((up, 1, (layer, fold, chip, span)))
    started = []
    for place, (origin, turn, index) in enumerate(copies):
        copy = pltpu.make_async_copy(origin, staged[turn].at[index], in_sems.at[place])
        copy.start()
        started.append(copy)
    for copy in started:
        copy.wait()
    ended = []
    for turn, (origin, target) in enumerate(zip(staged, targets)):
        copy = pltpu.make_async_copy(origin, target, out_sems.at[turn])
        copy.start()
        ended.append(copy)
    for copy in ended:
        copy.wait()


def place_blocks(pieces, where, form, shapes):
    plan = [(labels, first) for labels, first, _ in pieces]
    blocks = sum(len(labels) for labels, _, _ in pieces)
    copies = blocks * {"attention": 4, "first": 2, "second": 1, "adapter": 12}[form]
    anywhere = pl.BlockSpec(memory_space=pl.ANY)
    return pl.pallas_call(
        functools.partial(place_kernel, plan, form),
        grid_spec=pltpu.PrefetchScalarGridSpec(
            num_scalar_prefetch=1,
            grid=(1,),
            in_specs=[anywhere] * len(pieces),
            out_specs=[anywhere] * len(shapes),
            scratch_shapes=[pltpu.VMEM(shape, jnp.bfloat16) for shape in shapes]
            + [pltpu.SemaphoreType.DMA((copies,)), pltpu.SemaphoreType.DMA((len(shapes),))],
        ),
        out_shape=[jax.ShapeDtypeStruct(shape, jnp.bfloat16) for shape in shapes],
        compiler_params=pltpu.CompilerParams(vmem_limit_bytes=24 * MEBI),
        cost_estimate=LIGHT,
    )(where, *[stack for _, _, stack in pieces])


def head_scores(length, causal, query, keys):
    scores = times_second(query, keys) * score_scale
    key = lax.broadcasted_iota(jnp.int32, scores.shape, 1)
    mask = key < length
    if causal:
        mask = mask & (key <= lax.broadcasted_iota(jnp.int32, scores.shape, 0))
    return jnp.where(mask, scores, -1000000000.0)


def softmax(scores):
    weights = jnp.exp(scores - jnp.max(scores, 1, keepdims=True))
    return weights * (1.0 / jnp.sum(weights, 1, keepdims=True))


def one_head(value, head):
    lane = lax.broadcasted_iota(jnp.int32, value.shape, 1)
    return jnp.where(lane // HDIM == head, value, jnp.zeros((), value.dtype))


def attention_kernel(causal, length_ref, query_ref, key_ref, value_ref, out_ref):
    query, keys, values = query_ref[...], key_ref[...], value_ref[...]
    out = jnp.zeros(out_ref.shape, jnp.float32)
    for head in range(query.shape[1] // HDIM):
        scores = head_scores(length_ref[0], causal, query, one_head(keys, head))
        out = out + times_plain(bfloat(softmax(scores)), one_head(values, head))
    out_ref[...] = bfloat(out)


def attention_grad_kernel(
    causal, length_ref, query_ref, key_ref, value_ref, out_ref, query_out, key_out, value_out
):
    query, keys, values, out_grad = query_ref[...], key_ref[...], value_ref[...], out_ref[...]
    query_grad = jnp.zeros(query.shape, jnp.float32)
    key_grad = jnp.zeros(keys.shape, jnp.float32)
    value_grad = jnp.zeros(values.shape, jnp.float32)
    for head in range(query.shape[1] // HDIM):
        head_keys = one_head(keys, head)
        head_out = one_head(out_grad, head)
        probs = softmax(head_scores(length_ref[0], causal, query, head_keys))
        prob_grad = times_second(head_out, values)
        spread = jnp.sum(probs * prob_grad, 1, keepdims=True)
        score_grad = bfloat(probs * (prob_grad - spread))
        value_grad = value_grad + times_first(bfloat(probs), head_out)
        query_grad = query_grad + times_plain(score_grad, head_keys)
        key_grad = key_grad + times_first(score_grad, one_head(query, head))
    query_out[...] = bfloat(query_grad * score_scale)
    key_out[...] = bfloat(key_grad * score_scale)
    value_out[...] = bfloat(value_grad)


def attention_call(kernel, length, causal, arrays, outs):
    lanes = 2 * HDIM
    columns = outs[0][1]

    def spec(rows, first):
        return pl.BlockSpec((rows, lanes), lambda i, _: (0, i + first // lanes))

    return pl.pallas_call(
        functools.partial(kernel, causal),
        grid_spec=pltpu.PrefetchScalarGridSpec(
            num_scalar_prefetch=1,
            grid=(columns // lanes,),
            in_specs=[spec(array.shape[0], first) for array, first in arrays],
            out_specs=[spec(rows, 0) for rows, _ in outs],
        ),
        out_shape=[jax.ShapeDtypeStruct(out, jnp.bfloat16) for out in outs],
        compiler_params=pltpu.CompilerParams(vmem_limit_bytes=48 * MEBI),
        cost_estimate=LIGHT,
    )(length.reshape(1), *[array for array, _ in arrays])


def attend(length, causal, query, pair):
    rows = query[0].shape[0]
    width = pair[0].shape[1] - pair[1]
    half = width // 2
    arrays = [query, pair, (pair[0], pair[1] + half)]
    return attention_call(attention_kernel, length, causal, arrays, [(rows, half)])[0]


def attend_back(length, causal, query, pair, out_grad):
    rows = query[0].shape[0]
    keys = pair[0].shape[0]
    half = (pair[0].shape[1] - pair[1]) // 2
    arrays = [query, pair, (pair[0], pair[1] + half), (out_grad, 0)]
    outs = [(rows, half), (keys, half), (keys, half)]
    return attention_call(attention_grad_kernel, length, causal, arrays, outs)


def gelu_pair(value):
    phi = 0.5 * (1.0 + lax.erf(value * 0.7071067811865476))
    slope = phi + value * jnp.exp(-0.5 * value * value) * 0.3989422804014327
    return lax.optimization_barrier((bfloat(value * phi), slope))


def feed_forward(low_in, w_first, w_second, down, upward):
    hidden = times_plain(low_in, w_first)
    inner = times_plain(low_in, down)
    hidden_low, slope = gelu_pair(hidden)
    inner_low, inner_slope = gelu_pair(inner)
    branch = times_plain(hidden_low, w_second) + 4.0 * times_plain(inner_low, upward)
    return (branch, (low_in, slope, inner_slope, inner_low))


def feed_grad_kernel(grad_ref, second_ref, slope_ref, first_ref, out_ref):
    hidden_grad = bfloat(times_second(grad_ref[...], second_ref[...]) * slope_ref[...])
    part = times_second(hidden_grad, first_ref[...])

    @pl.when(pl.program_id(0) == 0)
    def _():
        out_ref[...] = part

    @pl.when(pl.program_id(0) > 0)
    def _():
        out_ref[...] += part


def feed_grad(grad, w_second, slope, w_first):
    rows, width = grad.shape
    units = w_second.shape[0]
    tile = min(units, 512)
    return pl.pallas_call(
        feed_grad_kernel,
        grid=(units // tile,),
        in_specs=[
            pl.BlockSpec((rows, width), lambda i: (0, 0)),
            pl.BlockSpec((tile, width), lambda i: (i, 0)),
            pl.BlockSpec((rows, tile), lambda i: (0, i)),
            pl.BlockSpec((width, tile), lambda i: (0, i)),
        ],
        out_specs=pl.BlockSpec((rows, width), lambda i: (0, 0)),
        out_shape=jax.ShapeDtypeStruct((rows, width), jnp.float32),
        compiler_params=pltpu.CompilerParams(vmem_limit_bytes=40 * MEBI),
        cost_estimate=LIGHT,
    )(grad, w_second, slope, w_first)


def feed_backward(grad, cache, w_first, w_second, down, upward):
    low_in, slope, inner_slope, inner_low = cache
    hidden_part = feed_grad(bfloat(grad), w_second, slope, w_first)
    adapter_grad = bfloat(4.0 * grad)
    upward_grad = times_first(inner_low, adapter_grad)
    inner_grad = bfloat(times_second(adapter_grad, upward) * inner_slope)
    down_grad = times_first(low_in, inner_grad)
    value_grad = hidden_part + times_second(inner_grad, down)
    return (value_grad, down_grad, upward_grad)


def vocab_kernel(
    count, tile, step, order_ref, rows_ref, table_ref, mixed_ref, stats_ref,
    scores, table, mixed, stats, table_sems, out_sems,
):
    parts = step // LIVE_ROWS
    turn = pl.program_id(0)
    alive = order_ref[order_ref.shape[0] - 1]
    padded = table.shape[0]
    tiles = range(0, padded, tile)

    def table_copy(place):
        span = slice(place * tile, (place + 1) * tile)
        return pltpu.make_async_copy(table_ref.at[span], table.at[span], table_sems.at[place])

    def out_copies(first):
        copies = []
        for part in range(parts):
            row = pl.multiple_of(order_ref[first + part] * LIVE_ROWS, LIVE_ROWS)
            span = slice(part * LIVE_ROWS, (part + 1) * LIVE_ROWS)
            for place, (origin, target) in enumerate(((mixed, mixed_ref), (stats, stats_ref))):
                copies.append(
                    pltpu.make_async_copy(
                        origin.at[span],
                        target.at[pl.ds(row, LIVE_ROWS)],
                        out_sems.at[place, part],
                    )
                )
        return copies

    @pl.when(turn == 0)
    def _():
        for place in range(len(tiles)):
            table_copy(place).start()
        for place in range(len(tiles)):
            table_copy(place).wait()

    first = turn * parts

    @pl.when(first < alive)
    def _():
        places = [
            pl.ds(pl.multiple_of(order_ref[first + part] * LIVE_ROWS, LIVE_ROWS), LIVE_ROWS)
            for part in range(parts)
        ]
        rows = jnp.concatenate([rows_ref[place, :] for place in places])
        top = jnp.full((step, 1), LOWEST, jnp.float32)
        for start in tiles:
            part = times_second(rows, table[start : start + tile, :])
            if start + tile > count:
                entry = lax.broadcasted_iota(jnp.int32, part.shape, 1) + start
                part = jnp.where(entry < count, part, LOWEST)
            scores[:, start : start + tile] = part
            top = jnp.maximum(top, jnp.max(part, 1, keepdims=True))
        total = jnp.zeros((step, 1), jnp.float32)
        mix = jnp.zeros((step, rows.shape[1]), jnp.float32)
        for start in tiles:
            weights = jnp.exp(scores[:, start : start + tile] - top)
            total = total + jnp.sum(weights, 1, keepdims=True)
            mix = mix + times_plain(bfloat(weights), table[start : start + tile, :])

        @pl.when(turn > 0)
        def _():
            for copy in out_copies(first - parts):
                copy.wait()

        mixed[...] = mix
        stats[...] = jnp.concatenate(
            [jnp.broadcast_to(top, (step, 64)), jnp.broadcast_to(total, (step, 64))], 1
        )
        for copy in out_copies(first):
            copy.start()

        @pl.when(first + parts >= alive)
        def _():
            for copy in out_copies(first):
                copy.wait()


def vocab_pass(rows, live_blocks, table, count, step, tile):
    total, width = rows.shape
    padded = table.shape[0]
    flags = live_blocks.astype(jnp.int32)
    alive_count = jnp.sum(flags)
    rank = jnp.where(
        live_blocks, jnp.cumsum(flags) - 1, alive_count + jnp.cumsum(1 - flags) - 1
    )
    ids = jnp.arange(flags.shape[0], dtype=jnp.int32)
    order = jnp.sum(jnp.where(rank[None, :] == ids[:, None], ids[None, :], 0), 1)
    order = jnp.concatenate([order, alive_count[None]]).astype(jnp.int32)

    anywhere = pl.BlockSpec(memory_space=pl.ANY)
    return pl.pallas_call(
        functools.partial(vocab_kernel, count, tile, step),
        grid_spec=pltpu.PrefetchScalarGridSpec(
            num_scalar_prefetch=1,
            grid=(total // step,),
            in_specs=[
                pl.BlockSpec((total, width), lambda i, _: (0, 0), pipeline_mode=pl.Buffered(1)),
                anywhere,
            ],
            out_specs=[anywhere, anywhere],
            scratch_shapes=[
                pltpu.VMEM((step, padded), jnp.float32),
                pltpu.VMEM((padded, width), jnp.bfloat16),
                pltpu.VMEM((step, width), jnp.float32),
                pltpu.VMEM((step, 128), jnp.float32),
                pltpu.SemaphoreType.DMA((padded // tile,)),
                pltpu.SemaphoreType.DMA((2, step // LIVE_ROWS)),
            ],
        ),
        out_shape=[
            jax.ShapeDtypeStruct((total, width), jnp.float32),
            jax.ShapeDtypeStruct((total, 128), jnp.float32),
        ],
        compiler_params=pltpu.CompilerParams(vmem_limit_bytes=56 * MEBI),
        cost_estimate=pl.CostEstimate(
            flops=3 * total * width * padded,
            bytes_accessed=2 * padded * width + 6 * total * width,
            transcendentals=total * padded,
        ),
    )(order, rows, table)


def exchange(values, bits):
    got = [swap(value, bit, 0) for value, bit in zip(values, bits)]
    return lax.optimization_barrier(got)


def spread(halves, orders):
    halves = [{0: half} for half in halves]
    for turn in range(len(orders[0])):
        keys = sorted(halves[0])
        got = exchange(
            [jnp.stack([half[k] for k in sorted(half)]) for half in halves],
            [bits[turn] for bits in orders],
        )
        halves = [
            half | {key | bits[turn]: other[place] for place, key in enumerate(sorted(half))}
            for half, other, bits in zip(halves, got, orders)
        ]
    return halves


def halved_steps(halves, orders):
    for turn in range(len(orders[0])):
        sent, kept = [], []
        for half, bits in zip(halves, orders):
            keep = [key for key in sorted(half) if not key & bits[turn]]
            kept.append(keep)
            away = jnp.stack([bfloat(half[key | bits[turn]]) for key in keep])
            sent += [swap(away, bits[turn], 0), jnp.stack([half[key] for key in keep])]
        done = yield sent
        halves = [
            {
                key: own[place].astype(jnp.float32) + got[place].astype(jnp.float32)
                for place, key in enumerate(keep)
            }
            for keep, got, own in zip(kept, done[::2], done[1::2])
        ]
    return [half[0] for half in halves]


def merged_sum(halves, orders):
    for turn in range(len(orders[0])):
        sent, kept = [], []
        for half, bits in zip(halves, orders):
            keep = [key for key in sorted(half) if not key & bits[turn]]
            kept.append(keep)
            away = [half[key | bits[turn]] for key in keep]
            sent.append(jnp.stack([bfloat(mix) for mix, _ in away]))
            sent.append(jnp.stack([stats for _, stats in away]))
        got = exchange(sent, [bits[turn] for bits in orders for _ in range(2)])
        merged = []
        for place, (half, keep) in enumerate(zip(halves, kept)):
            mixes, stats = got[2 * place], got[2 * place + 1]
            blocks = {}
            for index, key in enumerate(keep):
                mix, (top, total) = half[key]
                other_top, other_total = stats[index]
                best = jnp.maximum(top, other_top)
                scale = jnp.exp(top - best)
                other_scale = jnp.exp(other_top - best)
                mix = mix * scale[:, None] + mixes[index].astype(jnp.float32) * other_scale[:, None]
                total = total * scale + other_total * other_scale
                blocks[key] = (mix, jnp.stack([best, total]))
            merged.append(blocks)
        halves = merged
    return [half[0] for half in halves]


def fold_kernel(
    orders, where_ref, down_ref, other_ref, up_ref, *outs
):
    core, kind = where_ref[0], where_ref[1]
    chips, _, kv_count, _, lanes = down_ref.shape
    folds = up_ref.shape[-1] // lanes
    for task, bit in enumerate(orders):
        gate = (kind == task).astype(jnp.float32)
        place = where_ref[2 + task]
        keep_ref, send_ref = outs[2 * task], outs[2 * task + 1]
        pairs = [(high, low) for high in range(chips // (2 * bit)) for low in range(bit)]
        for index, (high, low) in enumerate(pairs):
            for side, out_ref in ((place, keep_ref), (1 - place, send_ref)):
                chip = (2 * high + side) * bit + low
                for z in range(kv_count):
                    up = up_ref[chip, z]
                    parts = [down_ref[chip, core, z], other_ref[chip, z].astype(jnp.float32)]
                    parts += [up[:, fold * lanes : (fold + 1) * lanes] for fold in range(folds)]
                    out_ref[index, z] = (jnp.concatenate(parts) * gate).astype(out_ref.dtype)


def halve_kernel(posts, where_ref, *refs):
    tasks = len(posts)
    for task, post in enumerate(posts):
        keep_ref, got_ref = refs[2 * task], refs[2 * task + 1]
        out_ref, send_ref = refs[2 * tasks + 2 * task], refs[2 * tasks + 2 * task + 1]
        place = where_ref[task]
        for high in range(keep_ref.shape[0] // (2 * post)):
            for low in range(post):
                for side, target in ((place, out_ref), (1 - place, send_ref)):
                    index = (2 * high + side) * post + low
                    total = keep_ref[index] + got_ref[index].astype(jnp.float32)
                    target[high * post + low] = total.astype(target.dtype)


def column_kernel(tasks, where_ref, *refs):
    own_ref, sends = refs[2 * tasks], refs[2 * tasks + 1 :]
    for task in range(tasks):
        keep_ref, got_ref = refs[2 * task], refs[2 * task + 1]
        for step, target in enumerate((own_ref,) + sends):
            z = where_ref[0] ^ step
            total = keep_ref[0, z] + got_ref[0, z].astype(jnp.float32)
            target[task] = total.astype(target.dtype)


def in_vmem(kernel, where, arrays, outs):
    whole = pl.BlockSpec(memory_space=pltpu.VMEM)
    return pl.pallas_call(
        kernel,
        in_specs=[pl.BlockSpec(memory_space=pltpu.SMEM)] + [whole] * len(arrays),
        out_specs=[whole] * len(outs),
        out_shape=[jax.ShapeDtypeStruct(shape, dtype) for shape, dtype in outs],
        compiler_params=pltpu.CompilerParams(vmem_limit_bytes=40 * MEBI),
        cost_estimate=LIGHT,
    )(jnp.stack(where).astype(jnp.int32), *arrays)


def adapter_steps(down_grad, up_grad, kind, tasks, lead):
    seq_count, kv_count = lax.axis_size("seq"), lax.axis_size("kv")
    seq_index, kv_index = lax.axis_index("seq"), lax.axis_index("kv")
    chips = seq_count // 2
    devices = seq_count * kv_count
    core = seq_index % 2
    lanes = down_grad.shape[1]
    down_rows = down_grad.shape[0] // devices
    up_rows = up_grad.shape[0] // (chips * kv_count)
    folds = up_grad.shape[1] // lanes
    height = 2 * down_rows + folds * up_rows
    down_part = down_grad.reshape(chips, 2, kv_count, down_rows, lanes)
    up_part = up_grad.reshape(chips, kv_count, up_rows, folds * lanes)
    down_part, other, up_part = yield [
        down_part,
        swap(bfloat(pick(down_part, 1, 1 - core)), 1, 0),
        up_part,
    ]
    x_bits, y_bits = plane_bits()
    orders = [(x_bits + y_bits, y_bits + x_bits)[task % 2] for task in range(tasks)]
    lefts = [sorted(x_bits + y_bits) for _ in range(tasks)]

    def shapes(count):
        shape = (count, kv_count, height, lanes)
        return [(shape, dtype) for _ in range(tasks) for dtype in (jnp.float32, jnp.bfloat16)]

    count = chips // 2
    parts = in_vmem(
        functools.partial(fold_kernel, [bits[0] // 2 for bits in orders]),
        [core, kind] + [(seq_index // bits[0]) % 2 for bits in orders],
        [down_part, other, up_part],
        shapes(count),
    )
    for turn in range(len(orders[0])):
        parts = list(parts)
        for task, bits in enumerate(orders):
            lefts[task].remove(bits[turn])
            parts[2 * task + 1] = swap(parts[2 * task + 1], bits[turn], 0)
        parts = yield parts
        if turn + 1 < len(orders[0]):
            count //= 2
            bits = [order[turn + 1] for order in orders]
            parts = in_vmem(
                functools.partial(
                    halve_kernel, [2 ** left.index(bit) for left, bit in zip(lefts, bits)]
                ),
                [(seq_index // bit) % 2 for bit in bits],
                parts,
                shapes(count),
            )
    shape = (tasks, height, lanes)
    outs = in_vmem(
        functools.partial(column_kernel, tasks),
        [kv_index],
        parts,
        [(shape, jnp.float32)] + [(shape, jnp.bfloat16)] * (kv_count - 1),
    )
    done = yield [outs[0]] + [swap(outs[step], 0, step) for step in range(1, kv_count)]
    total = done[0]
    for other in done[1:]:
        total = total + other.astype(jnp.float32)
    sides = in_order(core, total[:, :down_rows], total[:, down_rows : 2 * down_rows])
    sides = [
        side.reshape(tasks, down_rows, seq_count // (2 * lead), lanes * 2 * lead // seq_count)
        for side in sides
    ]
    down_total = jnp.stack(sides, 3).reshape(tasks, down_rows, 2 * lanes)
    up_total = total[:, 2 * down_rows :].reshape(tasks, folds, up_rows, lanes)
    up_total = up_total.transpose(0, 2, 1, 3).reshape(tasks, up_rows, folds * lanes)
    if lead == 2:
        up_total = trade_bits(up_total)
    return (down_total, up_total)


class Steps:
    def __init__(self, steps):
        self.steps = steps
        self.sent = next(steps)
        self.result = None

    def after(self, value):
        if self.result is not None:
            return
        count = len(self.sent)
        try:
            self.sent = self.steps.send(
                list(lax.optimization_barrier(tuple(self.sent) + (value,))[:count])
            )
        except StopIteration as stop:
            self.result = stop.value

    def along(self, values):
        count = len(self.sent)
        done = lax.optimization_barrier(tuple(self.sent) + tuple(values))
        if self.result is None:
            try:
                self.sent = self.steps.send(list(done[:count]))
            except StopIteration as stop:
                self.result, self.sent = stop.value, []
        return list(done[count:])

    def finish(self):
        while self.result is None:
            try:
                self.sent = self.steps.send(self.sent)
            except StopIteration as stop:
                self.result = stop.value
        return self.result


def total_sum(value):
    seq_count, kv_count = lax.axis_size("seq"), lax.axis_size("kv")
    value = value + swap(value, 1, 0)
    masks = [(bit, 0) for bit in sum(plane_bits(), [])]
    masks += [(0, 1 << place) for place in range(kv_count.bit_length() - 1)]
    for first, second in zip(masks[::2], masks[1::2]):
        both = (first[0] | second[0], first[1] | second[1])
        got = [swap(value, *mask) for mask in (first, second, both)]
        value = (value + got[0]) + (got[1] + got[2])
    return value


def half_rows(embeds):
    seq_count, kv_count = lax.axis_size("seq"), lax.axis_size("kv")
    kv_index = lax.axis_index("kv")
    got = []
    for turn in range(2):
        pairs = []
        for s in range(seq_count):
            for z in range(kv_count):
                source = (s - s % 2 + z % 2) * kv_count + 2 * (s % 2) + ((z // 2) ^ turn)
                pairs.append((source, s * kv_count + z))
        sent = pick(embeds[:, 0], 0, (kv_index % 2) ^ turn)
        got.append(lax.ppermute(sent, AXES, pairs))
    swapped = kv_index // 2 == 1
    return jnp.concatenate(
        [jnp.where(swapped, got[1], got[0]), jnp.where(swapped, got[0], got[1])]
    )


def adam_update(weight, first, second, grad, rate, decay, count_step):
    first_new = beta_one * first + (1.0 - beta_one) * grad
    second_new = beta_two * second + (1.0 - beta_two) * grad * grad
    first_hat = first_new / (1.0 - jnp.power(beta_one, count_step))
    second_hat = second_new / (1.0 - jnp.power(beta_two, count_step))
    weight_new = weight - rate * (
        first_hat / (jnp.sqrt(second_hat) + adam_epsilon) + decay * weight
    )
    return (weight_new, first_new, second_new)


def per_device(
    src_embed,
    tgt_embed,
    targets,
    src_len,
    tgt_len,
    task,
    step,
    attn_in,
    attn_out,
    ffn_in,
    ffn_out,
    embed,
    down_w,
    down_m,
    down_v,
    up_w,
    up_m,
    up_v,
    norm_params,
    norm_m,
    norm_v,
):
    seq_count, kv_count = lax.axis_size("seq"), lax.axis_size("kv")
    seq_index, kv_index = lax.axis_index("seq"), lax.axis_index("kv")
    chips = seq_count // 2
    devices = seq_count * kv_count
    width = attn_out.shape[2]
    hidden = ffn_in.shape[2]
    bottleneck = down_w.shape[3]
    tasks = down_w.shape[1]
    vocab_rows = embed.shape[0]
    vocab_total = vocab_rows * seq_count
    core = seq_index % 2
    batch = kv_index // 2
    item = seq_index - core + kv_index % 2
    source_length = src_len[batch, item]
    target_length = tgt_len[batch, item]
    kind = task[batch, item]
    count = jnp.sum(tgt_len).astype(jnp.float32)
    gains = norm_params[0]
    biases = norm_params[1]

    x_bits, y_bits = plane_bits()
    orders = (x_bits + y_bits, y_bits + x_bits)
    share = width // devices
    lead = 1 if kv_count * share % HDIM == 0 else 2
    sides = [
        core_columns(part, lead)
        for part in (
            [attn_in[j].reshape(share, 3, width) for j in range(3)]
            + [ffn_in[0], ffn_in[1]]
            + [bfloat(down_w[l, t]) for l in range(2) for t in range(tasks)]
        )
    ]
    flat = [jnp.concatenate([part[c].reshape(share, -1) for part in sides], 1) for c in range(2)]
    mine = jnp.where(core == 0, flat[0], flat[1])
    theirs = swap(jnp.where(core == 0, flat[1], flat[0]), 1, 0)
    split = jnp.stack(in_order(core, mine, theirs))
    edges = [0]
    for part in sides:
        edges.append(edges[-1] + part[0].size // share)
    split = [split[:, :, first:last] for first, last in zip(edges, edges[1:])]
    out_low, second_low, up_low = attn_out, ffn_out, bfloat(up_w)
    if lead == 2:
        out_low, second_low, up_low = trade_bits((out_low, second_low, up_low))
    half_w = width // 2
    own_attn = [
        jnp.concatenate(
            [split[j], out_low[j].reshape(share, 2, half_w).transpose(1, 0, 2)], 2
        )
        for j in range(3)
    ]
    lanes = bottleneck // 2
    up_rows = up_w.shape[2]
    own_down = jnp.stack(split[5:]).reshape(2 * tasks, 2, 2, share // 2, lanes)
    own_up = up_low.reshape(2 * tasks, up_rows, 4, lanes).transpose(0, 2, 1, 3)
    own_adapter = jnp.concatenate([own_down, own_up.reshape(2 * tasks, 2, 2, up_rows, lanes)])
    attn_shapes = [
        (chips, 2, kv_count, share, 3 * half_w),
        (2, chips, kv_count, share, half_w),
    ]
    first_shapes = [(chips, 2, kv_count, share, hidden // 2)]
    second_shapes = [(chips, kv_count, hidden // devices, width)]
    adapter_shapes = [
        (2, chips, 2, kv_count, 2, share // 2, lanes),
        (2, 4, chips, kv_count, up_rows, lanes),
    ]
    groups = [
        (second_low[0][None], "second", second_shapes),
        (own_attn[0], "attention", attn_shapes),
        (own_attn[1], "attention", attn_shapes),
        (split[3], "first", first_shapes),
        (own_adapter, "adapter", adapter_shapes),
        (own_attn[2], "attention", attn_shapes),
        (split[4], "first", first_shapes),
        (second_low[1][None], "second", second_shapes),
    ]
    where = jnp.stack([seq_index // 2, kind]).astype(jnp.int32)
    tile = 1280

    def column_start(place):
        return lambda made: [(place, column_first_steps(groups[place][0]))]

    def with_last(made):
        return [
            (len(groups) - 1, plane_first_steps(after(groups[-1][0], made["tie"]))),
            (2, column_first_steps(groups[2][0])),
        ]

    def ids_in(made):
        ids = after(targets, made["tie"])
        parts = [pick(ids, 0, batch)]
        for turn in range(1, kv_count):
            parts.append(swap(pick(ids, 0, batch ^ (turn // 2)), 0, turn))
        order = kv_index ^ jnp.arange(kv_count, dtype=jnp.int32)
        chosen = order[:, None] == jnp.arange(kv_count, dtype=jnp.int32)[None, :]
        parts = jnp.sum(jnp.where(chosen[:, :, None, None], jnp.stack(parts)[:, None], 0), 0)
        return {"ids": parts.transpose(1, 0, 2)}

    def rows_in(made):
        source, target = half_rows(src_embed), half_rows(tgt_embed)
        return {"half_rows": (source, target)}

    def whole_rows(made):
        source, target = [
            jnp.concatenate(in_order(core, half_item, swap(half_item, 1, 0)))
            for half_item in made["half_rows"]
        ]
        return {"source": source, "target": target}

    def table_in(made):
        low = after(embed, made["tie"])
        return {"table": jnp.pad(low, ((0, -vocab_rows % tile), (0, 0)))}

    def sum_in(made):
        return {"table_sum": jnp.sum(after(embed, made["tie"]).astype(jnp.float32), 0)}

    own_rows = tgt_embed.shape[2] * kv_count // 2
    half = own_rows // 2
    relative = seq_index ^ jnp.arange(seq_count, dtype=jnp.int32)
    row_items = relative - relative % 2 + kv_index % 2
    row_pos = (
        (relative % 2)[None, :, None] * own_rows
        + jnp.arange(2, dtype=jnp.int32)[:, None, None] * half
        + jnp.arange(half, dtype=jnp.int32)[None, None, :]
    )
    plane_lengths = pick(tgt_len, 0, batch)
    plane_lengths = jnp.sum(
        jnp.where(row_items[:, None] == jnp.arange(seq_count)[None, :], plane_lengths[None], 0), 1
    )
    alive = row_pos < plane_lengths[None, :, None]
    live = alive.astype(jnp.float32) / count

    def linear_in(made):
        ids = made["ids"].reshape(seq_count, 2, 2, half)
        chosen = (row_items[:, None] == jnp.arange(seq_count)[None, :])[:, :, None] & (
            (relative % 2)[:, None, None] == jnp.arange(2)[None, None, :]
        )
        row_ids = jnp.sum(jnp.where(chosen[:, :, :, None, None], ids[None], 0), (1, 2))
        row_ids = row_ids.transpose(1, 0, 2).reshape(-1)
        local_ids = after(row_ids - seq_index * vocab_rows, made["tie"])
        local_hit = (local_ids >= 0) & (local_ids < vocab_rows)
        target_rows = jnp.take(embed, jnp.clip(local_ids, 0, vocab_rows - 1), axis=0)
        linear = bfloat(
            jnp.where(local_hit[:, None], 0.9 * target_rows.astype(jnp.float32), 0.0)
            + (0.1 / vocab_total) * made["table_sum"][None]
        )
        return {"linear": linear.reshape(2, seq_count, half, width)}

    def last_in(made):
        return {"last": step + 0}

    starts = [column_start(place) for place in range(len(groups) - 1)]
    starts[2] = with_last
    def place(made, group):
        _, form, shape = groups[group]
        return place_blocks(made[group], where, form, shape)

    def attention_weights(made, group):
        w_in, w_out = place(made, group)
        w_out = jnp.concatenate(list(w_out.reshape(2, half_w, half_w)), 1)
        return (w_in.reshape(width, 3 * half_w), w_out)

    def encoder_attention(made):
        w_in, w_out = attention_weights(made, 1)
        x0, cache = norm_forward(made["source"].astype(jnp.float32), gains[0], biases[0])
        pair = bfloat(times_plain(bfloat(x0), w_in))
        out = attend(source_length, False, (pair, 0), (pair, half_w))
        return {
            "enc": (x0, cache, pair, times_plain(out, w_out)),
            "enc_w": (w_in, w_out),
        }

    def decoder_attention(made):
        x0, cache0, pair, part = made["enc"]
        x1, cache1 = norm_forward(x0 + core_sum(part), gains[1], biases[1])
        w_in, w_out = attention_weights(made, 2)
        y0, cache3 = norm_forward(made["target"].astype(jnp.float32), gains[3], biases[3])
        self_pair = bfloat(times_plain(bfloat(y0), w_in))
        out = attend(target_length, True, (self_pair, 0), (self_pair, half_w))
        return {
            "x1": (x1, cache1),
            "dec": (y0, cache3, self_pair, times_plain(out, w_out)),
            "dec_w": (w_in, w_out),
        }

    def encoder_hidden(made):
        y0, cache3, self_pair, part = made["dec"]
        y1, cache4 = norm_forward(y0 + core_sum(part), gains[4], biases[4])
        first = place(made, 3)[0].reshape(width, hidden // 2)
        low_in = bfloat(made["x1"][0])
        return {
            "y1": (y1, cache4),
            "first0": first,
            "hidden0": (low_in,) + gelu_pair(times_plain(low_in, first)),
        }

    def encoder_branch(made):
        down_all, up_all = place(made, 4)
        down_all = down_all.reshape(2, width, lanes)
        up_all = up_all.reshape(2, 4, lanes, lanes)
        up_all = jnp.concatenate([up_all[:, fold] for fold in range(4)], 2)
        second = place(made, 0)[0].reshape(hidden // 2, width)
        low_in, hidden_low, slope = made["hidden0"]
        inner_low, inner_slope = gelu_pair(times_plain(low_in, down_all[0]))
        part = times_plain(hidden_low, second) + 4.0 * times_plain(inner_low, up_all[0])
        return {
            "adapters": (down_all, up_all),
            "second0": second,
            "feed0": (part, (low_in, slope, inner_slope, inner_low)),
        }

    def cross_attention(made):
        x2, cache2 = norm_forward(made["x1"][0] + core_sum(made["feed0"][0]), gains[2], biases[2])
        w_in, w_out = attention_weights(made, 5)
        cross_query = bfloat(times_plain(bfloat(made["y1"][0]), w_in[:, :half_w]))
        cross_pair = bfloat(times_plain(bfloat(x2), w_in[:, half_w:]))
        out = attend(source_length, False, (cross_query, 0), (cross_pair, 0))
        return {
            "cross": (cache2, cross_query, cross_pair, times_plain(out, w_out)),
            "cross_w": (w_in, w_out),
        }

    extras = {
        0: rows_in,
        1: whole_rows,
        2: table_in,
        3: lambda made: sum_in(made) | ids_in(made),
        4: encoder_attention,
        5: decoder_attention,
        6: lambda made: encoder_hidden(made) | last_in(made),
        7: encoder_branch,
        8: cross_attention,
    }
    late = len(x_bits + y_bits) - 2
    extras = {turn + (late if turn > 3 else 0): value for turn, value in extras.items()}
    if late:
        extras[4] = linear_in
    else:
        attention_first = extras[4]
        extras[4] = lambda made: attention_first(made) | linear_in(made)
    gathered, made = run_rounds(starts, extras)
    table, linear = made["table"], made["linear"]
    x0, cache0, enc_pair, _ = made["enc"]
    x1, cache1 = made["x1"]
    y0, cache3, self_pair, _ = made["dec"]
    y1, cache4 = made["y1"]
    cache2, cross_query, cross_pair, part = made["cross"]
    down_all, up_all = made["adapters"]
    enc_feed = made["feed0"][1]
    attn_w = [made["enc_w"], made["dec_w"], made["cross_w"]]
    down_orders = [[1] + list(bits) for bits in orders]
    linear_steps = Steps(
        halved_steps(
            [
                {key: after(linear[h, key], made["tie"]) for key in range(seq_count)}
                for h in range(2)
            ],
            down_orders,
        )
    )
    y2, cache5 = norm_forward(y1 + core_sum(part), gains[5], biases[5])
    first_w = [made["first0"], place(gathered, 6)[0].reshape(width, hidden // 2)]
    labels, stack = gathered[len(groups) - 1]
    stack = lax.all_gather(after(stack, made["last"]), "kv", axis=1)
    second_w = place({7: [(labels, 0, stack)]}, 7)[0].reshape(hidden // 2, width)
    second_w = [made["second0"], second_w]
    branch, dec_feed = feed_forward(bfloat(y2), first_w[1], second_w[1], down_all[1], up_all[1])
    y3, cache6 = norm_forward(y2 + core_sum(branch), gains[6], biases[6])

    linear_steps.after(y2)
    y3_low = bfloat(y3)
    near = [
        lax.dynamic_slice_in_dim(y3_low, place * own_rows + h * half, half)
        for h in range(2)
        for place in (core, 1 - core)
    ]
    linear_steps.after(near[0])
    far = spread([near[0], near[2]], [list(bits) + [1] for bits in orders])
    near = jnp.concatenate(near)
    far = jnp.concatenate([half_far[key] for half_far in far for key in range(2, seq_count)])
    blocks = [{}, {}]
    loss_part = 0.0
    for rows, first, last in ((near, 0, 2), (far, 2, seq_count)):
        flags = jnp.any(alive[:, first:last].reshape(-1, LIVE_ROWS), 1)
        mixed, stats = vocab_pass(rows, flags, table, vocab_rows, 256, tile)
        mixed = mixed.reshape(2, last - first, half, width)
        tops = stats[:, 0].reshape(2, last - first, half)
        totals = stats[:, 64].reshape(2, last - first, half)
        for h in range(2):
            for key in range(first, last):
                pair = jnp.stack([tops[h, key - first], totals[h, key - first]])
                blocks[h][key] = (mixed[h, key - first], pair)
    linear_sum = linear_steps.finish()
    merged = merged_sum(blocks, down_orders)
    final_grad = []
    for h, (mix, (top, total)) in enumerate(merged):
        row_grad = (mix / total[:, None] - linear_sum[h]) * live[h, 0][:, None]
        final_grad.append(jnp.where(alive[h, 0][:, None], row_grad, 0.0))
        loss_part = loss_part + jnp.sum(jnp.where(alive[h, 0], top + jnp.log(total), 0.0))
    final_grad = bfloat(jnp.concatenate(final_grad))
    final_grad = jnp.concatenate(in_order(core, final_grad, swap(final_grad, 1, 0)))
    final_grad = final_grad.astype(jnp.float32)

    grad, grad6 = norm_backward(final_grad, cache6, gains[6])
    inner_grad, down_grad, up_grad = feed_backward(
        grad, dec_feed, first_w[1], second_w[1], down_all[1], up_all[1]
    )
    tied = lax.optimization_barrier
    inner_grad, down_grad, up_grad = tied((inner_grad, down_grad, up_grad))
    dec_steps = Steps(adapter_steps(down_grad, up_grad, kind, tasks, lead))
    grad, grad5 = norm_backward(grad + core_sum(inner_grad), cache5, gains[5])
    out_grad = bfloat(times_second(bfloat(grad), attn_w[2][1]))
    dq, dk, dv = attend_back(source_length, False, (cross_query, 0), (cross_pair, 0), out_grad)
    enc_grad = times_second(jnp.concatenate([dk, dv], 1), attn_w[2][0][:, half_w:])
    query_grad = times_second(dq, attn_w[2][0][:, :half_w])
    (part,) = dec_steps.along([jnp.concatenate([enc_grad, query_grad])])
    summed = core_sum(part)
    enc_rows = x0.shape[0]
    dec_grad, grad4 = norm_backward(grad + summed[enc_rows:], cache4, gains[4])
    grad, grad2 = norm_backward(summed[:enc_rows], cache2, gains[2])
    inner_grad, down_grad, up_grad = feed_backward(
        grad, enc_feed, first_w[0], second_w[0], down_all[0], up_all[0]
    )
    inner_grad, down_grad, up_grad, dec_grad, grad = dec_steps.along(
        [inner_grad, down_grad, up_grad, dec_grad, grad]
    )
    enc_steps = Steps(adapter_steps(down_grad, up_grad, kind, tasks, lead))
    inner_sum = core_sum(inner_grad)
    out_grad = bfloat(times_second(bfloat(dec_grad), attn_w[1][1]))
    parts = attend_back(target_length, True, (self_pair, 0), (self_pair, half_w), out_grad)
    part = times_second(jnp.concatenate(parts, 1), attn_w[1][0])
    part, inner_sum, *sent = dec_steps.along([part, inner_sum] + enc_steps.sent)
    enc_steps.sent = sent
    part, inner_sum = enc_steps.along([part, inner_sum])
    self_sum = core_sum(part)
    grad, grad1 = norm_backward(grad + inner_sum, cache1, gains[1])
    out_grad = bfloat(times_second(bfloat(grad), attn_w[0][1]))
    parts = attend_back(source_length, False, (enc_pair, 0), (enc_pair, half_w), out_grad)
    part = times_second(jnp.concatenate(parts, 1), attn_w[0][0])
    part, self_sum, grad = enc_steps.along([part, self_sum, grad])
    enc_sum = core_sum(part)
    _, grad3 = norm_backward(dec_grad + self_sum, cache3, gains[3])
    (enc_sum,) = enc_steps.along([enc_sum])
    _, grad0 = norm_backward(grad + enc_sum, cache0, gains[0])
    enc_sums, dec_sums = enc_steps.finish(), dec_steps.finish()

    linear = after(linear, enc_sum)
    for rows, first, last in ((near, 0, 2), (far, 2, seq_count)):
        rows = rows.astype(jnp.float32).reshape(2, last - first, half, width)
        rows_alive = alive[:, first:last].astype(jnp.float32)[..., None]
        loss_part = loss_part - jnp.sum(rows_alive * rows * linear[:, first:last].astype(jnp.float32))

    norm_grad = 0.5 * jnp.stack([grad0, grad1, grad2, grad3, grad4, grad5, grad6], 1)
    down_part = jnp.stack([enc_sums[0], dec_sums[0]])
    up_part = jnp.stack([enc_sums[1], dec_sums[1]])
    square = jnp.sum(down_part * down_part) + jnp.sum(up_part * up_part)
    scalars = jnp.zeros((1, width), jnp.float32).at[0, 0].set(loss_part).at[0, 1].set(square)
    summed = total_sum(jnp.concatenate([norm_grad.reshape(-1, width), scalars]))
    norm_sum = summed[:-1].reshape(norm_grad.shape)
    loss_sum = summed[-1, 0]
    grad_norm = jnp.sqrt(summed[-1, 1] + jnp.sum(norm_sum * norm_sum))
    factor = clip_limit / jnp.maximum(grad_norm, clip_limit)
    count_step = step[0].astype(jnp.float32)
    down_new = adam_update(
        down_w, down_m, down_v, factor * down_part, rate_adapter, weight_decay, count_step
    )
    up_new = adam_update(up_w, up_m, up_v, factor * up_part, rate_adapter, weight_decay, count_step)
    norm_grad_out = factor * norm_sum
    norm_new = adam_update(norm_params, norm_m, norm_v, norm_grad_out, rate_norm, 0.0, count_step)
    return (
        loss_sum,
        count,
        grad_norm,
        down_new[0],
        down_new[1],
        down_new[2],
        up_new[0],
        up_new[1],
        up_new[2],
        norm_new[0],
        norm_new[1],
        norm_new[2],
        norm_grad_out,
    )


def solution(mesh):
    placed = (
        P(None, "seq", "kv", None),
        P(None, "seq", "kv", None),
        P(None, None, "kv"),
        P(),
        P(),
        P(),
        P(),
        P(None, ("seq", "kv"), None),
        P(None, ("seq", "kv"), None),
        P(None, ("seq", "kv"), None),
        P(None, ("seq", "kv"), None),
        P("seq", None),
        P(None, None, ("seq", "kv"), None),
        P(None, None, ("seq", "kv"), None),
        P(None, None, ("seq", "kv"), None),
        P(None, None, ("seq", "kv"), None),
        P(None, None, ("seq", "kv"), None),
        P(None, None, ("seq", "kv"), None),
        P(),
        P(),
        P(),
    )
    return jax.shard_map(
        per_device,
        mesh=mesh,
        in_specs=placed,
        out_specs=(
            P(),
            P(),
            P(),
            P(None, None, ("seq", "kv"), None),
            P(None, None, ("seq", "kv"), None),
            P(None, None, ("seq", "kv"), None),
            P(None, None, ("seq", "kv"), None),
            P(None, None, ("seq", "kv"), None),
            P(None, None, ("seq", "kv"), None),
            P(),
            P(),
            P(),
            P(),
        ),
        check_vma=False,
    )
```

```python
import functools

import jax
import jax.numpy as jnp
from jax import lax
from jax.experimental import pallas as pl
from jax.experimental.pallas import tpu as pltpu
from jax.sharding import PartitionSpec as P

HDIM = 64


norm_epsilon = 1e-05
score_scale = 0.125
clip_limit = 0.02
beta_one = 0.9
beta_two = 0.999
adam_epsilon = 1e-08
rate_adapter = 0.03
rate_norm = 0.25
weight_decay = 0.01


def bfloat(value):
    return value.astype(jnp.bfloat16)


def times_plain(left, right):
    return jnp.dot(left, right, preferred_element_type=jnp.float32)


def times_first(left, right):
    return lax.dot_general(
        left, right, (((0,), (0,)), ((), ())), preferred_element_type=jnp.float32
    )


def times_second(left, right):
    return lax.dot_general(
        left, right, (((1,), (1,)), ((), ())), preferred_element_type=jnp.float32
    )


def norm_forward(value, gain, bias):
    centered = value - jnp.mean(value, -1, keepdims=True)
    inverse = lax.rsqrt(jnp.mean(centered * centered, -1, keepdims=True) + norm_epsilon)
    normed = centered * inverse
    return (normed * gain + bias, (normed, inverse))


def norm_backward(grad, cache, gain):
    normed, inverse = cache
    scaled = grad * gain
    value_grad = inverse * (
        scaled
        - jnp.mean(scaled, -1, keepdims=True)
        - normed * jnp.mean(scaled * normed, -1, keepdims=True)
    )
    return (value_grad, jnp.stack([jnp.sum(grad * normed, 0), jnp.sum(grad, 0)]))


def gelu_slope(value):
    return (
        0.5 * (1.0 + lax.erf(value * 0.7071067811865476))
        + value * jnp.exp(-0.5 * value * value) * 0.3989422804014327
    )


AXES = ("seq", "kv")
MEBI = 2**20
LOWEST = -3e38
LIVE_ROWS = 64
LIGHT = pl.CostEstimate(flops=1, bytes_accessed=1, transcendentals=0)


def swap(value, seq_mask, kv_mask):
    seq_count, kv_count = lax.axis_size("seq"), lax.axis_size("kv")
    pairs = [
        (s * kv_count + z, (s ^ seq_mask) * kv_count + (z ^ kv_mask))
        for s in range(seq_count)
        for z in range(kv_count)
    ]
    return lax.ppermute(value, AXES, pairs)


def trade_bits(value):
    seq_count, kv_count = lax.axis_size("seq"), lax.axis_size("kv")
    pairs = [
        (s * kv_count + z, (s - s % 4 + 2 * (s % 2) + s // 2 % 2) * kv_count + z)
        for s in range(seq_count)
        for z in range(kv_count)
    ]
    return lax.ppermute(value, AXES, pairs)


def plane_bits():
    count = lax.axis_size("seq").bit_length() - 2
    bits = [2 << place for place in range(count)]
    return (bits[: count // 2], bits[count // 2 :])


def after(value, earlier):
    return lax.optimization_barrier((value, earlier))[0]


def pick(value, axis, index):
    return lax.dynamic_index_in_dim(value, index, axis, keepdims=False)


def in_order(core, mine, other):
    first = core == 0
    return (jnp.where(first, mine, other), jnp.where(first, other, mine))


def core_sum(value):
    return value + swap(bfloat(value), 1, 0).astype(jnp.float32)


def core_columns(value, lead):
    seq_count = lax.axis_size("seq")
    total = value.shape[-1]
    chunk = total // seq_count
    parts = value.reshape(value.shape[:-1] + (seq_count // (2 * lead), 2, lead * chunk))
    flat = value.shape[:-1] + (total // 2,)
    return (parts[..., 0, :].reshape(flat), parts[..., 1, :].reshape(flat))


def plane_steps(stacks, orders, firsts):
    labels = [[0] for _ in stacks]
    for turn in range(len(orders[0])):
        got = [swap(stack, bits[turn], 0) for stack, bits in zip(stacks, orders)]
        done = yield list(stacks) + got
        stacks, got = done[: len(stacks)], done[len(stacks) :]
        fresh = [[label | bits[turn] for label in old] for old, bits in zip(labels, orders)]
        if turn == len(orders[0]) - 1:
            break
        stacks = [jnp.concatenate(pair) for pair in zip(stacks, got)]
        labels = [old + new for old, new in zip(labels, fresh)]
    return [
        piece
        for old, new, first, stack, other in zip(labels, fresh, firsts, stacks, got)
        for piece in ((old, first, stack), (new, first, other))
    ]


def column_first_steps(own):
    (column,) = yield [lax.all_gather(own, "kv")]
    half = column.shape[0] // 2
    x_bits, y_bits = plane_bits()
    orders = (x_bits + y_bits, y_bits + x_bits)
    return (yield from plane_steps([column[None, :half], column[None, half:]], orders, (0, half)))


def plane_first_steps(own):
    x_bits, y_bits = plane_bits()
    half = own.shape[1] // 2
    orders = (x_bits + y_bits, y_bits + x_bits)
    parts = [own[None, None, :, :half], own[None, None, :, half:]]
    pieces = yield from plane_steps(parts, orders, (0, 0))
    stacks = []
    for first, second in (pieces[:2], pieces[2:]):
        labels = first[0] + second[0]
        stack = jnp.concatenate([first[2], second[2]])[:, 0]
        stacks.append(jnp.stack([stack[labels.index(label)] for label in sorted(labels)]))
    return (sorted(labels), jnp.concatenate(stacks, 2))


def run_rounds(starts, extras):
    live = {}
    results = {}
    turn = 0
    made = {}
    while turn < len(starts) or live:
        if turn < len(starts):
            for name, steps in starts[turn](made):
                live[name] = (steps, None)
        values, spans = [], {}
        for name, (steps, sent) in list(live.items()):
            try:
                out = steps.send(sent)
            except StopIteration as stop:
                results[name] = stop.value
                made[name] = stop.value
                del live[name]
                continue
            spans[name] = (len(values), len(values) + len(out))
            values += out
        if not values:
            turn += 1
            continue
        more = extras.get(turn, lambda made: {})(made)
        names = list(more)
        leaves, shape = jax.tree.flatten([more[name] for name in names])
        values = lax.optimization_barrier(tuple(values) + tuple(leaves))
        for name, (first, last) in spans.items():
            live[name] = (live[name][0], list(values[first:last]))
        made.update(zip(names, jax.tree.unflatten(shape, values[len(values) - len(leaves) :])))
        made["tie"] = values[0]
        turn += 1
    return results, made


def place_kernel(plan, form, where_ref, *refs):
    sources = refs[: len(plan)]
    count = (len(refs) - len(plan) - 2) // 2
    targets = refs[len(plan) : len(plan) + count]
    staged = refs[len(plan) + count : len(plan) + 2 * count]
    in_sems, out_sems = refs[-2:]
    own = where_ref[0]
    kind = where_ref[1]
    copies = []
    for source, (labels, first) in zip(sources, plan):
        for place, label in enumerate(labels):
            chip = own ^ (label // 2)
            block = source.at[place]
            span = slice(first, first + source.shape[1])
            if form == "attention":
                split = staged[0].shape[-1]
                for side in range(2):
                    copies.append((block.at[:, side, :, :split], 0, (chip, side, span)))
                    copies.append((block.at[:, side, :, split:], 1, (side, chip, span)))
            elif form == "first":
                for side in range(2):
                    copies.append((block.at[:, side], 0, (chip, side, span)))
            elif form == "second":
                copies.append((block.at[:, 0], 0, (chip, span)))
            else:
                for layer in range(2):
                    for side in range(2):
                        down = block.at[:, 2 * layer + kind, side]
                        copies.append((down, 0, (layer, chip, side, span)))
                    for fold in range(4):
                        up = block.at[:, 4 + 2 * layer + kind, fold // 2, fold % 2]
                        copies.append((up, 1, (layer, fold, chip, span)))
    started = []
    for place, (origin, turn, index) in enumerate(copies):
        copy = pltpu.make_async_copy(origin, staged[turn].at[index], in_sems.at[place])
        copy.start()
        started.append(copy)
    for copy in started:
        copy.wait()
    ended = []
    for turn, (origin, target) in enumerate(zip(staged, targets)):
        copy = pltpu.make_async_copy(origin, target, out_sems.at[turn])
        copy.start()
        ended.append(copy)
    for copy in ended:
        copy.wait()


def place_blocks(pieces, where, form, shapes):
    plan = [(labels, first) for labels, first, _ in pieces]
    blocks = sum(len(labels) for labels, _, _ in pieces)
    copies = blocks * {"attention": 4, "first": 2, "second": 1, "adapter": 12}[form]
    anywhere = pl.BlockSpec(memory_space=pl.ANY)
    return pl.pallas_call(
        functools.partial(place_kernel, plan, form),
        grid_spec=pltpu.PrefetchScalarGridSpec(
            num_scalar_prefetch=1,
            grid=(1,),
            in_specs=[anywhere] * len(pieces),
            out_specs=[anywhere] * len(shapes),
            scratch_shapes=[pltpu.VMEM(shape, jnp.bfloat16) for shape in shapes]
            + [pltpu.SemaphoreType.DMA((copies,)), pltpu.SemaphoreType.DMA((len(shapes),))],
        ),
        out_shape=[jax.ShapeDtypeStruct(shape, jnp.bfloat16) for shape in shapes],
        compiler_params=pltpu.CompilerParams(vmem_limit_bytes=24 * MEBI),
        cost_estimate=LIGHT,
    )(where, *[stack for _, _, stack in pieces])


def head_scores(length, causal, query, keys):
    scores = times_second(query, keys) * score_scale
    key = lax.broadcasted_iota(jnp.int32, scores.shape, 1)
    mask = key < length
    if causal:
        mask = mask & (key <= lax.broadcasted_iota(jnp.int32, scores.shape, 0))
    return jnp.where(mask, scores, -1000000000.0)


def softmax(scores):
    weights = jnp.exp(scores - jnp.max(scores, 1, keepdims=True))
    return weights * (1.0 / jnp.sum(weights, 1, keepdims=True))


def one_head(value, head):
    lane = lax.broadcasted_iota(jnp.int32, value.shape, 1)
    return jnp.where(lane // HDIM == head, value, jnp.zeros((), value.dtype))


def attention_kernel(causal, length_ref, query_ref, key_ref, value_ref, out_ref):
    query, keys, values = query_ref[...], key_ref[...], value_ref[...]
    out = jnp.zeros(out_ref.shape, jnp.float32)
    for head in range(query.shape[1] // HDIM):
        scores = head_scores(length_ref[0], causal, query, one_head(keys, head))
        out = out + times_plain(bfloat(softmax(scores)), one_head(values, head))
    out_ref[...] = bfloat(out)


def attention_grad_kernel(
    causal, length_ref, query_ref, key_ref, value_ref, out_ref, query_out, key_out, value_out
):
    query, keys, values, out_grad = query_ref[...], key_ref[...], value_ref[...], out_ref[...]
    query_grad = jnp.zeros(query.shape, jnp.float32)
    key_grad = jnp.zeros(keys.shape, jnp.float32)
    value_grad = jnp.zeros(values.shape, jnp.float32)
    for head in range(query.shape[1] // HDIM):
        head_keys = one_head(keys, head)
        head_out = one_head(out_grad, head)
        probs = softmax(head_scores(length_ref[0], causal, query, head_keys))
        prob_grad = times_second(head_out, values)
        spread = jnp.sum(probs * prob_grad, 1, keepdims=True)
        score_grad = bfloat(probs * (prob_grad - spread))
        value_grad = value_grad + times_first(bfloat(probs), head_out)
        query_grad = query_grad + times_plain(score_grad, head_keys)
        key_grad = key_grad + times_first(score_grad, one_head(query, head))
    query_out[...] = bfloat(query_grad * score_scale)
    key_out[...] = bfloat(key_grad * score_scale)
    value_out[...] = bfloat(value_grad)


def attention_call(kernel, length, causal, arrays, outs):
    lanes = 2 * HDIM
    columns = outs[0][1]

    def spec(rows, first):
        return pl.BlockSpec((rows, lanes), lambda i, _: (0, i + first // lanes))

    return pl.pallas_call(
        functools.partial(kernel, causal),
        grid_spec=pltpu.PrefetchScalarGridSpec(
            num_scalar_prefetch=1,
            grid=(columns // lanes,),
            in_specs=[spec(array.shape[0], first) for array, first in arrays],
            out_specs=[spec(rows, 0) for rows, _ in outs],
        ),
        out_shape=[jax.ShapeDtypeStruct(out, jnp.bfloat16) for out in outs],
        compiler_params=pltpu.CompilerParams(vmem_limit_bytes=48 * MEBI),
        cost_estimate=LIGHT,
    )(length.reshape(1), *[array for array, _ in arrays])


def attend(length, causal, query, pair):
    rows = query[0].shape[0]
    width = pair[0].shape[1] - pair[1]
    half = width // 2
    arrays = [query, pair, (pair[0], pair[1] + half)]
    return attention_call(attention_kernel, length, causal, arrays, [(rows, half)])[0]


def attend_back(length, causal, query, pair, out_grad):
    rows = query[0].shape[0]
    keys = pair[0].shape[0]
    half = (pair[0].shape[1] - pair[1]) // 2
    arrays = [query, pair, (pair[0], pair[1] + half), (out_grad, 0)]
    outs = [(rows, half), (keys, half), (keys, half)]
    return attention_call(attention_grad_kernel, length, causal, arrays, outs)


def gelu_pair(value):
    phi = 0.5 * (1.0 + lax.erf(value * 0.7071067811865476))
    slope = phi + value * jnp.exp(-0.5 * value * value) * 0.3989422804014327
    return lax.optimization_barrier((bfloat(value * phi), slope))


def feed_forward(low_in, w_first, w_second, down, upward):
    hidden = times_plain(low_in, w_first)
    inner = times_plain(low_in, down)
    hidden_low, slope = gelu_pair(hidden)
    inner_low, inner_slope = gelu_pair(inner)
    branch = times_plain(hidden_low, w_second) + 4.0 * times_plain(inner_low, upward)
    return (branch, (low_in, slope, inner_slope, inner_low))


def feed_grad_kernel(grad_ref, second_ref, slope_ref, first_ref, out_ref):
    hidden_grad = bfloat(times_second(grad_ref[...], second_ref[...]) * slope_ref[...])
    part = times_second(hidden_grad, first_ref[...])

    @pl.when(pl.program_id(0) == 0)
    def _():
        out_ref[...] = part

    @pl.when(pl.program_id(0) > 0)
    def _():
        out_ref[...] += part


def feed_grad(grad, w_second, slope, w_first):
    rows, width = grad.shape
    units = w_second.shape[0]
    tile = min(units, 512)
    return pl.pallas_call(
        feed_grad_kernel,
        grid=(units // tile,),
        in_specs=[
            pl.BlockSpec((rows, width), lambda i: (0, 0)),
            pl.BlockSpec((tile, width), lambda i: (i, 0)),
            pl.BlockSpec((rows, tile), lambda i: (0, i)),
            pl.BlockSpec((width, tile), lambda i: (0, i)),
        ],
        out_specs=pl.BlockSpec((rows, width), lambda i: (0, 0)),
        out_shape=jax.ShapeDtypeStruct((rows, width), jnp.float32),
        compiler_params=pltpu.CompilerParams(vmem_limit_bytes=40 * MEBI),
        cost_estimate=LIGHT,
    )(grad, w_second, slope, w_first)


def feed_backward(grad, cache, w_first, w_second, down, upward):
    low_in, slope, inner_slope, inner_low = cache
    hidden_part = feed_grad(bfloat(grad), w_second, slope, w_first)
    adapter_grad = bfloat(4.0 * grad)
    upward_grad = times_first(inner_low, adapter_grad)
    inner_grad = bfloat(times_second(adapter_grad, upward) * inner_slope)
    down_grad = times_first(low_in, inner_grad)
    value_grad = hidden_part + times_second(inner_grad, down)
    return (value_grad, down_grad, upward_grad)


def vocab_kernel(
    count, tile, step, order_ref, rows_ref, table_ref, mixed_ref, stats_ref,
    scores, table, mixed, stats, table_sems, out_sems,
):
    parts = step // LIVE_ROWS
    turn = pl.program_id(0)
    alive = order_ref[order_ref.shape[0] - 1]
    padded = table.shape[0]
    tiles = range(0, padded, tile)

    def table_copy(place):
        span = slice(place * tile, (place + 1) * tile)
        return pltpu.make_async_copy(table_ref.at[span], table.at[span], table_sems.at[place])

    def out_copies(first):
        copies = []
        for part in range(parts):
            row = pl.multiple_of(order_ref[first + part] * LIVE_ROWS, LIVE_ROWS)
            span = slice(part * LIVE_ROWS, (part + 1) * LIVE_ROWS)
            for place, (origin, target) in enumerate(((mixed, mixed_ref), (stats, stats_ref))):
                copies.append(
                    pltpu.make_async_copy(
                        origin.at[span],
                        target.at[pl.ds(row, LIVE_ROWS)],
                        out_sems.at[place, part],
                    )
                )
        return copies

    @pl.when(turn == 0)
    def _():
        for place in range(len(tiles)):
            table_copy(place).start()
        for place in range(len(tiles)):
            table_copy(place).wait()

    first = turn * parts

    @pl.when(first < alive)
    def _():
        places = [
            pl.ds(pl.multiple_of(order_ref[first + part] * LIVE_ROWS, LIVE_ROWS), LIVE_ROWS)
            for part in range(parts)
        ]
        rows = jnp.concatenate([rows_ref[place, :] for place in places])
        top = jnp.full((step, 1), LOWEST, jnp.float32)
        for start in tiles:
            part = times_second(rows, table[start : start + tile, :])
            if start + tile > count:
                entry = lax.broadcasted_iota(jnp.int32, part.shape, 1) + start
                part = jnp.where(entry < count, part, LOWEST)
            scores[:, start : start + tile] = part
            top = jnp.maximum(top, jnp.max(part, 1, keepdims=True))
        total = jnp.zeros((step, 1), jnp.float32)
        mix = jnp.zeros((step, rows.shape[1]), jnp.float32)
        for start in tiles:
            weights = jnp.exp(scores[:, start : start + tile] - top)
            total = total + jnp.sum(weights, 1, keepdims=True)
            mix = mix + times_plain(bfloat(weights), table[start : start + tile, :])

        @pl.when(turn > 0)
        def _():
            for copy in out_copies(first - parts):
                copy.wait()

        mixed[...] = mix
        stats[...] = jnp.concatenate(
            [jnp.broadcast_to(top, (step, 64)), jnp.broadcast_to(total, (step, 64))], 1
        )
        for copy in out_copies(first):
            copy.start()

        @pl.when(first + parts >= alive)
        def _():
            for copy in out_copies(first):
                copy.wait()


def vocab_pass(rows, live_blocks, table, count, step, tile):
    total, width = rows.shape
    padded = table.shape[0]
    flags = live_blocks.astype(jnp.int32)
    alive_count = jnp.sum(flags)
    rank = jnp.where(
        live_blocks, jnp.cumsum(flags) - 1, alive_count + jnp.cumsum(1 - flags) - 1
    )
    ids = jnp.arange(flags.shape[0], dtype=jnp.int32)
    order = jnp.sum(jnp.where(rank[None, :] == ids[:, None], ids[None, :], 0), 1)
    order = jnp.concatenate([order, alive_count[None]]).astype(jnp.int32)

    anywhere = pl.BlockSpec(memory_space=pl.ANY)
    return pl.pallas_call(
        functools.partial(vocab_kernel, count, tile, step),
        grid_spec=pltpu.PrefetchScalarGridSpec(
            num_scalar_prefetch=1,
            grid=(total // step,),
            in_specs=[
                pl.BlockSpec((total, width), lambda i, _: (0, 0), pipeline_mode=pl.Buffered(1)),
                anywhere,
            ],
            out_specs=[anywhere, anywhere],
            scratch_shapes=[
                pltpu.VMEM((step, padded), jnp.float32),
                pltpu.VMEM((padded, width), jnp.bfloat16),
                pltpu.VMEM((step, width), jnp.float32),
                pltpu.VMEM((step, 128), jnp.float32),
                pltpu.SemaphoreType.DMA((padded // tile,)),
                pltpu.SemaphoreType.DMA((2, step // LIVE_ROWS)),
            ],
        ),
        out_shape=[
            jax.ShapeDtypeStruct((total, width), jnp.float32),
            jax.ShapeDtypeStruct((total, 128), jnp.float32),
        ],
        compiler_params=pltpu.CompilerParams(vmem_limit_bytes=56 * MEBI),
        cost_estimate=pl.CostEstimate(
            flops=3 * total * width * padded,
            bytes_accessed=2 * padded * width + 6 * total * width,
            transcendentals=total * padded,
        ),
    )(order, rows, table)


def exchange(values, bits):
    got = [swap(value, bit, 0) for value, bit in zip(values, bits)]
    return lax.optimization_barrier(got)


def spread(halves, orders):
    halves = [{0: half} for half in halves]
    for turn in range(len(orders[0])):
        keys = sorted(halves[0])
        got = exchange(
            [jnp.stack([half[k] for k in sorted(half)]) for half in halves],
            [bits[turn] for bits in orders],
        )
        halves = [
            half | {key | bits[turn]: other[place] for place, key in enumerate(sorted(half))}
            for half, other, bits in zip(halves, got, orders)
        ]
    return halves


def halved_sum(halves, orders):
    for turn in range(len(orders[0])):
        sent, kept = [], []
        for half, bits in zip(halves, orders):
            keep = [key for key in sorted(half) if not key & bits[turn]]
            kept.append(keep)
            sent.append(jnp.stack([bfloat(half[key | bits[turn]]) for key in keep]))
        got = exchange(sent, [bits[turn] for bits in orders])
        halves = [
            {key: half[key] + other[place].astype(jnp.float32) for place, key in enumerate(keep)}
            for half, keep, other in zip(halves, kept, got)
        ]
    return [half[0] for half in halves]


def merged_sum(halves, orders):
    for turn in range(len(orders[0])):
        sent, kept = [], []
        for half, bits in zip(halves, orders):
            keep = [key for key in sorted(half) if not key & bits[turn]]
            kept.append(keep)
            away = [half[key | bits[turn]] for key in keep]
            sent.append(jnp.stack([bfloat(mix) for mix, _ in away]))
            sent.append(jnp.stack([stats for _, stats in away]))
        got = exchange(sent, [bits[turn] for bits in orders for _ in range(2)])
        merged = []
        for place, (half, keep) in enumerate(zip(halves, kept)):
            mixes, stats = got[2 * place], got[2 * place + 1]
            blocks = {}
            for index, key in enumerate(keep):
                mix, (top, total) = half[key]
                other_top, other_total = stats[index]
                best = jnp.maximum(top, other_top)
                scale = jnp.exp(top - best)
                other_scale = jnp.exp(other_top - best)
                mix = mix * scale[:, None] + mixes[index].astype(jnp.float32) * other_scale[:, None]
                total = total * scale + other_total * other_scale
                blocks[key] = (mix, jnp.stack([best, total]))
            merged.append(blocks)
        halves = merged
    return [half[0] for half in halves]


def adapter_steps(down_grad, up_grad, kind, tasks, lead):
    seq_count, kv_count = lax.axis_size("seq"), lax.axis_size("kv")
    seq_index, kv_index = lax.axis_index("seq"), lax.axis_index("kv")
    chips = seq_count // 2
    devices = seq_count * kv_count
    core = seq_index % 2
    lanes = down_grad.shape[1]
    down_rows = down_grad.shape[0] // devices
    up_rows = up_grad.shape[0] // (chips * kv_count)
    folds = up_grad.shape[1] // lanes
    down_part = down_grad.reshape(chips, 2, kv_count, down_rows, lanes)
    up_part = up_grad.reshape(chips, kv_count, up_rows, folds, lanes).transpose(0, 1, 3, 2, 4)
    up_part = up_part.reshape(chips, kv_count, folds * up_rows, lanes)
    mine, other, up_part = yield [
        pick(down_part, 1, core),
        swap(bfloat(pick(down_part, 1, 1 - core)), 1, 0),
        up_part,
    ]
    grad = jnp.concatenate([mine, other.astype(jnp.float32), up_part], 2)
    height = grad.shape[2]
    x_bits, y_bits = plane_bits()
    orders = [(x_bits + y_bits, y_bits + x_bits)[task % 2] for task in range(tasks)]
    lefts = [list(reversed(x_bits + y_bits)) for _ in range(tasks)]
    parts = []
    for task in range(tasks):
        part = grad * (kind == task).astype(jnp.float32)
        parts.append(
            part.reshape([2] * (len(x_bits) + len(y_bits)) + [kv_count, height, lanes])
        )
    for turn in range(len(orders[0])):
        kept, got = [], []
        for part, bits, left in zip(parts, orders, lefts):
            bit = bits[turn]
            axis = left.index(bit)
            left.remove(bit)
            place = (seq_index // bit) % 2
            kept.append(pick(part, axis, place))
            got.append(swap(bfloat(pick(part, axis, 1 - place)), bit, 0))
        done = yield kept + got
        parts = [
            part + other.astype(jnp.float32) for part, other in zip(done[:tasks], done[tasks:])
        ]
    part = jnp.stack(parts, 1)
    done = yield [pick(part, 0, kv_index)] + [
        swap(bfloat(pick(part, 0, kv_index ^ step)), 0, step) for step in range(1, kv_count)
    ]
    total = done[0]
    for other in done[1:]:
        total = total + other.astype(jnp.float32)
    sides = in_order(core, total[:, :down_rows], total[:, down_rows : 2 * down_rows])
    sides = [
        side.reshape(tasks, down_rows, seq_count // (2 * lead), lanes * 2 * lead // seq_count)
        for side in sides
    ]
    down_total = jnp.stack(sides, 3).reshape(tasks, down_rows, 2 * lanes)
    up_total = total[:, 2 * down_rows :].reshape(tasks, folds, up_rows, lanes)
    up_total = up_total.transpose(0, 2, 1, 3).reshape(tasks, up_rows, folds * lanes)
    if lead == 2:
        up_total = trade_bits(up_total)
    return (down_total, up_total)


class Steps:
    def __init__(self, steps):
        self.steps = steps
        self.sent = next(steps)
        self.result = None

    def after(self, value):
        if self.result is not None:
            return
        count = len(self.sent)
        try:
            self.sent = self.steps.send(
                list(lax.optimization_barrier(tuple(self.sent) + (value,))[:count])
            )
        except StopIteration as stop:
            self.result = stop.value

    def finish(self):
        while self.result is None:
            try:
                self.sent = self.steps.send(self.sent)
            except StopIteration as stop:
                self.result = stop.value
        return self.result


def total_sum(value):
    step = 1
    while step < lax.axis_size("seq"):
        value = value + swap(value, step, 0)
        step *= 2
    step = 1
    while step < lax.axis_size("kv"):
        value = value + swap(value, 0, step)
        step *= 2
    return value


def item_rows(embeds):
    seq_count, kv_count = lax.axis_size("seq"), lax.axis_size("kv")
    seq_index, kv_index = lax.axis_index("seq"), lax.axis_index("kv")
    got = []
    for turn in range(2):
        pairs = []
        for s in range(seq_count):
            for z in range(kv_count):
                source = (s - s % 2 + z % 2) * kv_count + 2 * (s % 2) + ((z // 2) ^ turn)
                pairs.append((source, s * kv_count + z))
        sent = pick(embeds[:, 0], 0, (kv_index % 2) ^ turn)
        got.append(lax.ppermute(sent, AXES, pairs))
    swapped = kv_index // 2 == 1
    mine = jnp.concatenate(
        [jnp.where(swapped, got[1], got[0]), jnp.where(swapped, got[0], got[1])]
    )
    return jnp.concatenate(in_order(seq_index % 2, mine, swap(mine, 1, 0)))


def adam_update(weight, first, second, grad, rate, decay, count_step):
    first_new = beta_one * first + (1.0 - beta_one) * grad
    second_new = beta_two * second + (1.0 - beta_two) * grad * grad
    first_hat = first_new / (1.0 - jnp.power(beta_one, count_step))
    second_hat = second_new / (1.0 - jnp.power(beta_two, count_step))
    weight_new = weight - rate * (
        first_hat / (jnp.sqrt(second_hat) + adam_epsilon) + decay * weight
    )
    return (weight_new, first_new, second_new)


def per_device(
    src_embed,
    tgt_embed,
    targets,
    src_len,
    tgt_len,
    task,
    step,
    attn_in,
    attn_out,
    ffn_in,
    ffn_out,
    embed,
    down_w,
    down_m,
    down_v,
    up_w,
    up_m,
    up_v,
    norm_params,
    norm_m,
    norm_v,
):
    seq_count, kv_count = lax.axis_size("seq"), lax.axis_size("kv")
    seq_index, kv_index = lax.axis_index("seq"), lax.axis_index("kv")
    chips = seq_count // 2
    devices = seq_count * kv_count
    width = attn_out.shape[2]
    hidden = ffn_in.shape[2]
    bottleneck = down_w.shape[3]
    tasks = down_w.shape[1]
    vocab_rows = embed.shape[0]
    vocab_total = vocab_rows * seq_count
    core = seq_index % 2
    batch = kv_index // 2
    item = seq_index - core + kv_index % 2
    source_length = src_len[batch, item]
    target_length = tgt_len[batch, item]
    kind = task[batch, item]
    count = jnp.sum(tgt_len).astype(jnp.float32)
    gains = norm_params[0]
    biases = norm_params[1]

    x_bits, y_bits = plane_bits()
    orders = (x_bits + y_bits, y_bits + x_bits)
    share = width // devices
    lead = 1 if kv_count * share % HDIM == 0 else 2
    sides = [
        core_columns(part, lead)
        for part in (
            [attn_in[j].reshape(share, 3, width) for j in range(3)]
            + [ffn_in[0], ffn_in[1]]
            + [bfloat(down_w[l, t]) for l in range(2) for t in range(tasks)]
        )
    ]
    flat = [jnp.concatenate([part[c].reshape(share, -1) for part in sides], 1) for c in range(2)]
    mine = jnp.where(core == 0, flat[0], flat[1])
    theirs = swap(jnp.where(core == 0, flat[1], flat[0]), 1, 0)
    split = jnp.stack(in_order(core, mine, theirs))
    edges = [0]
    for part in sides:
        edges.append(edges[-1] + part[0].size // share)
    split = [split[:, :, first:last] for first, last in zip(edges, edges[1:])]
    out_low, second_low, up_low = attn_out, ffn_out, bfloat(up_w)
    if lead == 2:
        out_low, second_low, up_low = trade_bits((out_low, second_low, up_low))
    half_w = width // 2
    own_attn = [
        jnp.concatenate(
            [split[j], out_low[j].reshape(share, 2, half_w).transpose(1, 0, 2)], 2
        )
        for j in range(3)
    ]
    lanes = bottleneck // 2
    up_rows = up_w.shape[2]
    own_down = jnp.stack(split[5:]).reshape(2 * tasks, 2, 2, share // 2, lanes)
    own_up = up_low.reshape(2 * tasks, up_rows, 4, lanes).transpose(0, 2, 1, 3)
    own_adapter = jnp.concatenate([own_down, own_up.reshape(2 * tasks, 2, 2, up_rows, lanes)])
    attn_shapes = [
        (chips, 2, kv_count, share, 3 * half_w),
        (2, chips, kv_count, share, half_w),
    ]
    first_shapes = [(chips, 2, kv_count, share, hidden // 2)]
    second_shapes = [(chips, kv_count, hidden // devices, width)]
    adapter_shapes = [
        (2, chips, 2, kv_count, 2, share // 2, lanes),
        (2, 4, chips, kv_count, up_rows, lanes),
    ]
    groups = [
        (second_low[0][None], "second", second_shapes),
        (own_attn[0], "attention", attn_shapes),
        (own_attn[1], "attention", attn_shapes),
        (split[3], "first", first_shapes),
        (own_adapter, "adapter", adapter_shapes),
        (own_attn[2], "attention", attn_shapes),
        (split[4], "first", first_shapes),
        (second_low[1][None], "second", second_shapes),
    ]
    where = jnp.stack([seq_index // 2, kind]).astype(jnp.int32)
    tile = 1280

    def column_start(place):
        return lambda made: [(place, column_first_steps(groups[place][0]))]

    def with_last(made):
        return [
            (len(groups) - 1, plane_first_steps(groups[-1][0])),
            (0, column_first_steps(groups[0][0])),
        ]

    def ids_in(made):
        parts = [pick(targets, 0, batch)]
        for turn in range(1, kv_count):
            parts.append(swap(pick(targets, 0, batch ^ (turn // 2)), 0, turn))
        order = kv_index ^ jnp.arange(kv_count, dtype=jnp.int32)
        chosen = order[:, None] == jnp.arange(kv_count, dtype=jnp.int32)[None, :]
        parts = jnp.sum(jnp.where(chosen[:, :, None, None], jnp.stack(parts)[:, None], 0), 0)
        return {"ids": parts.transpose(1, 0, 2)}

    def rows_in(made):
        return {
            "source": item_rows(src_embed),
            "target": item_rows(tgt_embed),
        }

    def table_in(made):
        low = after(embed, made["tie"])
        return {"table": jnp.pad(low, ((0, -vocab_rows % tile), (0, 0)))}

    def sum_in(made):
        return {"table_sum": jnp.sum(after(embed, made["tie"]).astype(jnp.float32), 0)}

    own_rows = tgt_embed.shape[2] * kv_count // 2
    half = own_rows // 2
    relative = seq_index ^ jnp.arange(seq_count, dtype=jnp.int32)
    row_items = relative - relative % 2 + kv_index % 2
    row_pos = (
        (relative % 2)[None, :, None] * own_rows
        + jnp.arange(2, dtype=jnp.int32)[:, None, None] * half
        + jnp.arange(half, dtype=jnp.int32)[None, None, :]
    )
    plane_lengths = pick(tgt_len, 0, batch)
    plane_lengths = jnp.sum(
        jnp.where(row_items[:, None] == jnp.arange(seq_count)[None, :], plane_lengths[None], 0), 1
    )
    alive = row_pos < plane_lengths[None, :, None]
    live = alive.astype(jnp.float32) / count

    def linear_in(made):
        ids = made["ids"].reshape(seq_count, 2, 2, half)
        chosen = (row_items[:, None] == jnp.arange(seq_count)[None, :])[:, :, None] & (
            (relative % 2)[:, None, None] == jnp.arange(2)[None, None, :]
        )
        row_ids = jnp.sum(jnp.where(chosen[:, :, :, None, None], ids[None], 0), (1, 2))
        row_ids = row_ids.transpose(1, 0, 2).reshape(-1)
        local_ids = after(row_ids - seq_index * vocab_rows, made["tie"])
        local_hit = (local_ids >= 0) & (local_ids < vocab_rows)
        target_rows = jnp.take(embed, jnp.clip(local_ids, 0, vocab_rows - 1), axis=0)
        linear = bfloat(
            jnp.where(local_hit[:, None], 0.9 * target_rows.astype(jnp.float32), 0.0)
            + (0.1 / vocab_total) * made["table_sum"][None]
        )
        return {"linear": linear.reshape(2, seq_count, half, width)}

    def last_in(made):
        return {"last": step + 0}

    starts = [with_last] + [column_start(place) for place in range(1, len(groups) - 1)]
    def place(made, group):
        _, form, shape = groups[group]
        return place_blocks(made[group], where, form, shape)

    def attention_weights(made, group):
        w_in, w_out = place(made, group)
        w_out = jnp.concatenate(list(w_out.reshape(2, half_w, half_w)), 1)
        return (w_in.reshape(width, 3 * half_w), w_out)

    def encoder_attention(made):
        w_in, w_out = attention_weights(made, 1)
        x0, cache = norm_forward(made["source"].astype(jnp.float32), gains[0], biases[0])
        pair = bfloat(times_plain(bfloat(x0), w_in))
        out = attend(source_length, False, (pair, 0), (pair, half_w))
        return {
            "enc": (x0, cache, pair, times_plain(out, w_out)),
            "enc_w": (w_in, w_out),
        }

    def decoder_attention(made):
        x0, cache0, pair, part = made["enc"]
        x1, cache1 = norm_forward(x0 + core_sum(part), gains[1], biases[1])
        w_in, w_out = attention_weights(made, 2)
        y0, cache3 = norm_forward(made["target"].astype(jnp.float32), gains[3], biases[3])
        self_pair = bfloat(times_plain(bfloat(y0), w_in))
        out = attend(target_length, True, (self_pair, 0), (self_pair, half_w))
        return {
            "x1": (x1, cache1),
            "dec": (y0, cache3, self_pair, times_plain(out, w_out)),
            "dec_w": (w_in, w_out),
        }

    def encoder_hidden(made):
        y0, cache3, self_pair, part = made["dec"]
        y1, cache4 = norm_forward(y0 + core_sum(part), gains[4], biases[4])
        first = place(made, 3)[0].reshape(width, hidden // 2)
        low_in = bfloat(made["x1"][0])
        return {
            "y1": (y1, cache4),
            "first0": first,
            "hidden0": (low_in,) + gelu_pair(times_plain(low_in, first)),
        }

    def encoder_branch(made):
        down_all, up_all = place(made, 4)
        down_all = down_all.reshape(2, width, lanes)
        up_all = up_all.reshape(2, 4, lanes, lanes)
        up_all = jnp.concatenate([up_all[:, fold] for fold in range(4)], 2)
        second = place(made, 0)[0].reshape(hidden // 2, width)
        low_in, hidden_low, slope = made["hidden0"]
        inner_low, inner_slope = gelu_pair(times_plain(low_in, down_all[0]))
        part = times_plain(hidden_low, second) + 4.0 * times_plain(inner_low, up_all[0])
        return {
            "adapters": (down_all, up_all),
            "second0": second,
            "feed0": (part, (low_in, slope, inner_slope, inner_low)),
        }

    def cross_attention(made):
        x2, cache2 = norm_forward(made["x1"][0] + core_sum(made["feed0"][0]), gains[2], biases[2])
        w_in, w_out = attention_weights(made, 5)
        cross_query = bfloat(times_plain(bfloat(made["y1"][0]), w_in[:, :half_w]))
        cross_pair = bfloat(times_plain(bfloat(x2), w_in[:, half_w:]))
        out = attend(source_length, False, (cross_query, 0), (cross_pair, 0))
        return {
            "cross": (cache2, cross_query, cross_pair, times_plain(out, w_out)),
            "cross_w": (w_in, w_out),
        }

    extras = {
        0: rows_in,
        1: ids_in,
        2: table_in,
        3: sum_in,
        4: encoder_attention,
        5: decoder_attention,
        6: lambda made: encoder_hidden(made) | last_in(made),
        7: encoder_branch,
        8: cross_attention,
    }
    late = len(x_bits + y_bits) - 2
    extras = {turn + (late if turn > 3 else 0): value for turn, value in extras.items()}
    if late:
        extras[4] = linear_in
    else:
        attention_first = extras[4]
        extras[4] = lambda made: attention_first(made) | linear_in(made)
    gathered, made = run_rounds(starts, extras)
    table, linear = made["table"], made["linear"]
    x0, cache0, enc_pair, _ = made["enc"]
    x1, cache1 = made["x1"]
    y0, cache3, self_pair, _ = made["dec"]
    y1, cache4 = made["y1"]
    cache2, cross_query, cross_pair, part = made["cross"]
    down_all, up_all = made["adapters"]
    enc_feed = made["feed0"][1]
    attn_w = [made["enc_w"], made["dec_w"], made["cross_w"]]
    y2, cache5 = norm_forward(y1 + core_sum(part), gains[5], biases[5])
    first_w = [made["first0"], place(gathered, 6)[0].reshape(width, hidden // 2)]
    labels, stack = gathered[len(groups) - 1]
    stack = lax.all_gather(after(stack, made["last"]), "kv", axis=1)
    second_w = place({7: [(labels, 0, stack)]}, 7)[0].reshape(hidden // 2, width)
    second_w = [made["second0"], second_w]
    branch, dec_feed = feed_forward(bfloat(y2), first_w[1], second_w[1], down_all[1], up_all[1])
    y3, cache6 = norm_forward(y2 + core_sum(branch), gains[6], biases[6])

    down_orders = [[1] + list(bits) for bits in orders]
    linear_sum = halved_sum(
        [
            {key: after(linear[h, key], made["tie"]) for key in range(seq_count)}
            for h in range(2)
        ],
        down_orders,
    )
    y3_low = bfloat(y3)
    near = [
        lax.dynamic_slice_in_dim(y3_low, place * own_rows + h * half, half)
        for h in range(2)
        for place in (core, 1 - core)
    ]
    far = spread([near[0], near[2]], [list(bits) + [1] for bits in orders])
    near = jnp.concatenate(near)
    far = jnp.concatenate([half_far[key] for half_far in far for key in range(2, seq_count)])
    blocks = [{}, {}]
    loss_part = 0.0
    for rows, first, last in ((near, 0, 2), (far, 2, seq_count)):
        flags = jnp.any(alive[:, first:last].reshape(-1, LIVE_ROWS), 1)
        mixed, stats = vocab_pass(rows, flags, table, vocab_rows, 256, tile)
        mixed = mixed.reshape(2, last - first, half, width)
        tops = stats[:, 0].reshape(2, last - first, half)
        totals = stats[:, 64].reshape(2, last - first, half)
        for h in range(2):
            for key in range(first, last):
                pair = jnp.stack([tops[h, key - first], totals[h, key - first]])
                blocks[h][key] = (mixed[h, key - first], pair)
        rows_alive = alive[:, first:last].astype(jnp.float32)[..., None]
        rows = rows.astype(jnp.float32).reshape(mixed.shape)
        loss_part = loss_part - jnp.sum(rows_alive * rows * linear[:, first:last].astype(jnp.float32))
    merged = merged_sum(blocks, down_orders)
    final_grad = []
    for h, (mix, (top, total)) in enumerate(merged):
        row_grad = (mix / total[:, None] - linear_sum[h]) * live[h, 0][:, None]
        final_grad.append(jnp.where(alive[h, 0][:, None], row_grad, 0.0))
        loss_part = loss_part + jnp.sum(jnp.where(alive[h, 0], top + jnp.log(total), 0.0))
    final_grad = bfloat(jnp.concatenate(final_grad))
    final_grad = jnp.concatenate(in_order(core, final_grad, swap(final_grad, 1, 0)))
    final_grad = final_grad.astype(jnp.float32)

    grad, grad6 = norm_backward(final_grad, cache6, gains[6])
    inner_grad, down_grad, up_grad = feed_backward(
        grad, dec_feed, first_w[1], second_w[1], down_all[1], up_all[1]
    )
    dec_steps = Steps(adapter_steps(down_grad, up_grad, kind, tasks, lead))
    grad, grad5 = norm_backward(grad + core_sum(inner_grad), cache5, gains[5])
    out_grad = bfloat(times_second(bfloat(grad), attn_w[2][1]))
    dec_steps.after(out_grad)
    dq, dk, dv = attend_back(source_length, False, (cross_query, 0), (cross_pair, 0), out_grad)
    enc_grad = times_second(jnp.concatenate([dk, dv], 1), attn_w[2][0][:, half_w:])
    query_grad = times_second(dq, attn_w[2][0][:, :half_w])
    dec_steps.after(dq)
    summed = core_sum(jnp.concatenate([enc_grad, query_grad]))
    enc_rows = x0.shape[0]
    dec_grad, grad4 = norm_backward(grad + summed[enc_rows:], cache4, gains[4])
    grad, grad2 = norm_backward(summed[:enc_rows], cache2, gains[2])
    inner_grad, down_grad, up_grad = feed_backward(
        grad, enc_feed, first_w[0], second_w[0], down_all[0], up_all[0]
    )
    dec_steps.after(inner_grad)
    enc_steps = Steps(adapter_steps(down_grad, up_grad, kind, tasks, lead))
    out_grad = bfloat(times_second(bfloat(dec_grad), attn_w[1][1]))
    parts = attend_back(target_length, True, (self_pair, 0), (self_pair, half_w), out_grad)
    enc_steps.after(out_grad)
    dec_steps.after(parts[0])
    self_grad = times_second(jnp.concatenate(parts, 1), attn_w[1][0])
    enc_steps.after(parts[0])
    _, grad3 = norm_backward(dec_grad + core_sum(self_grad), cache3, gains[3])
    grad, grad1 = norm_backward(grad + core_sum(inner_grad), cache1, gains[1])
    out_grad = bfloat(times_second(bfloat(grad), attn_w[0][1]))
    parts = attend_back(source_length, False, (enc_pair, 0), (enc_pair, half_w), out_grad)
    enc_steps.after(parts[0])
    enc_grad = times_second(jnp.concatenate(parts, 1), attn_w[0][0])
    _, grad0 = norm_backward(grad + core_sum(enc_grad), cache0, gains[0])
    enc_sums, dec_sums = enc_steps.finish(), dec_steps.finish()

    norm_grad = 0.5 * jnp.stack([grad0, grad1, grad2, grad3, grad4, grad5, grad6], 1)
    down_part = jnp.stack([enc_sums[0], dec_sums[0]])
    up_part = jnp.stack([enc_sums[1], dec_sums[1]])
    square = jnp.sum(down_part * down_part) + jnp.sum(up_part * up_part)
    scalars = jnp.zeros((1, width), jnp.float32).at[0, 0].set(loss_part).at[0, 1].set(square)
    summed = total_sum(jnp.concatenate([norm_grad.reshape(-1, width), scalars]))
    norm_sum = summed[:-1].reshape(norm_grad.shape)
    loss_sum = summed[-1, 0]
    grad_norm = jnp.sqrt(summed[-1, 1] + jnp.sum(norm_sum * norm_sum))
    factor = clip_limit / jnp.maximum(grad_norm, clip_limit)
    count_step = step[0].astype(jnp.float32)
    down_new = adam_update(
        down_w, down_m, down_v, factor * down_part, rate_adapter, weight_decay, count_step
    )
    up_new = adam_update(up_w, up_m, up_v, factor * up_part, rate_adapter, weight_decay, count_step)
    norm_grad_out = factor * norm_sum
    norm_new = adam_update(norm_params, norm_m, norm_v, norm_grad_out, rate_norm, 0.0, count_step)
    return (
        loss_sum,
        count,
        grad_norm,
        down_new[0],
        down_new[1],
        down_new[2],
        up_new[0],
        up_new[1],
        up_new[2],
        norm_new[0],
        norm_new[1],
        norm_new[2],
        norm_grad_out,
    )


def solution(mesh):
    placed = (
        P(None, "seq", "kv", None),
        P(None, "seq", "kv", None),
        P(None, None, "kv"),
        P(),
        P(),
        P(),
        P(),
        P(None, ("seq", "kv"), None),
        P(None, ("seq", "kv"), None),
        P(None, ("seq", "kv"), None),
        P(None, ("seq", "kv"), None),
        P("seq", None),
        P(None, None, ("seq", "kv"), None),
        P(None, None, ("seq", "kv"), None),
        P(None, None, ("seq", "kv"), None),
        P(None, None, ("seq", "kv"), None),
        P(None, None, ("seq", "kv"), None),
        P(None, None, ("seq", "kv"), None),
        P(),
        P(),
        P(),
    )
    return jax.shard_map(
        per_device,
        mesh=mesh,
        in_specs=placed,
        out_specs=(
            P(),
            P(),
            P(),
            P(None, None, ("seq", "kv"), None),
            P(None, None, ("seq", "kv"), None),
            P(None, None, ("seq", "kv"), None),
            P(None, None, ("seq", "kv"), None),
            P(None, None, ("seq", "kv"), None),
            P(None, None, ("seq", "kv"), None),
            P(),
            P(),
            P(),
            P(),
        ),
        check_vma=False,
    )
```
